128 devices in a mesh: rep: 8 (over y, core), sp: 16 (over z, x).
Axes of the slice: x: 4, y: 4, z: 4, core: 2. Of those that a mesh axis runs over, the one named last changes fastest.
Arguments:
- coords: float32 [8, 8192, 3, 128], P('rep', 'sp'), may hold values from -6 to 6
- atom_weight: float32 [8192, 128], P('sp'), may hold values from 0.005 to 0.05
- centers: float32 [512, 3, 128], P('sp'), may hold values from -6 to 6
- inv_width: float32 [512, 128], P('sp'), may hold values from 0.1 to 0.5
- density: float32 [512, 128], P('sp'), may hold values from 0 to 4
- variance: float32 [512, 128], P('sp'), may hold values from 1 to 4
- tile_blocks: int32 [512, 32], P('sp'), may hold values from 0 to 767, as said below
- tile_counts: int32 [512], P('sp'), may hold values from 20 to 32
- send_blocks: int32 [16, 16, 16], P('sp'), may hold values from 0 to 511, as said below
Outputs:
- forces: float32 [8, 8192, 3, 128], P('rep', 'sp')
- mean_model: float32 [512, 128], P('sp')
The draws below stay inside these ranges and needn't reach their ends.
Inputs may be any that keep to these rules, and one draw needn't show every extreme that they name: Within one list of send_blocks the 16 block numbers differ. `tile_blocks`: within one tile's list the entries differ. Among the live entries of a device's tiles every own block is named, and every received entry 512 + s * 16 + k whose source s differs from the owner's index, cyclically, by 1 to 16 / 4 - 1 or by exactly 16 / 2; no other received entry is named anywhere.
All inputs are finite; a program needn't handle non-finite values.
Results may differ from the reference program's by a relative error of at most 0.0003.
Values sent between devices are 32-bit elements; how exact they have to be, the bound alone decides.
A program may use at most 128 MiB of HBM per device.

```python
import math
import jax
import jax.numpy as jnp
from jax import lax

BLK_DEV = 512
TILE_DEV = 32
CAP = 16
MAXB = 32
REPLICAS = 8
BLOCKS = 8192
TILES = 512
N_REP = 8
N_SP = 16


def draw_send_blocks(key, part):
    scores = jax.random.randint(key, (N_SP, N_SP, BLK_DEV), 0, 1048576)
    order_ids = jnp.arange(BLK_DEV, dtype=jnp.int32)
    keyed_scores = scores * BLK_DEV + order_ids[None, None, :]
    first_pair = (jnp.arange(N_SP)[:, None, None] == 0) & (jnp.arange(N_SP)[None, :, None] == 1)
    keyed_scores = jnp.where(first_pair & (order_ids[None, None, :] == 0), -2, keyed_scores)
    keyed_scores = jnp.where(first_pair & (order_ids[None, None, :] == BLK_DEV - 1), -1, keyed_scores)
    ranked = jnp.argsort(keyed_scores, axis=-1, stable=True)
    return ranked[:, :, :CAP].astype(jnp.int32)


def item_count():
    return BLK_DEV + (N_SP // 2 - 1) * CAP


def draw_tile_blocks(key, part):
    items = item_count()
    stride_len = (items + TILE_DEV - 1) // TILE_DEV
    near_count = N_SP // 4 - 1
    scores = jax.random.randint(key, (N_SP, items), 0, 1048576)
    keyed_scores = scores * items + jnp.arange(items, dtype=jnp.int32)[None, :]
    shuffled = jnp.argsort(keyed_scores, axis=-1, stable=True).astype(jnp.int32)
    item_ids = jnp.arange(items, dtype=jnp.int32)
    rest_ids = jnp.maximum(item_ids - BLK_DEV, 0)
    neighbour = rest_ids // CAP
    within = rest_ids % CAP
    offsets = jnp.where(neighbour < near_count, neighbour + 1, jnp.where(neighbour < 2 * near_count, -(neighbour - near_count + 1), N_SP // 2))
    devices = jnp.arange(N_SP, dtype=jnp.int32)[:, None]
    sources = (devices + offsets[None, :] + N_SP) % N_SP
    values = jnp.where(item_ids[None, :] < BLK_DEV, item_ids[None, :], BLK_DEV + sources * CAP + within[None, :]).astype(jnp.int32)
    position_ids = (stride_len * jnp.arange(TILE_DEV, dtype=jnp.int32)[:, None] + jnp.arange(MAXB, dtype=jnp.int32)[None, :]) % items
    picked = shuffled[:, position_ids]
    tile_lists = jnp.take_along_axis(values, picked.reshape(N_SP, TILE_DEV * MAXB), axis=1)
    return tile_lists.reshape(N_SP * TILE_DEV, MAXB).astype(jnp.int32)


def draw_tile_counts(key, part):
    items = item_count()
    stride_len = (items + TILE_DEV - 1) // TILE_DEV
    lowest = min(stride_len, MAXB)
    key_top, key_each, key_pick = jax.random.split(key, 3)
    device_top = jax.random.randint(key_top, (N_SP, 1), lowest, MAXB + 1)
    counts_raw = jax.random.randint(key_each, (N_SP, TILE_DEV), lowest, device_top + 1)
    tile_total = N_SP * TILE_DEV
    flat_counts = counts_raw.reshape(tile_total)
    picked = jax.random.randint(key_pick, (), 0, tile_total)
    positions = jnp.arange(tile_total, dtype=jnp.int32)
    flat_counts = jnp.where(positions == picked, MAXB, flat_counts)
    flat_counts = jnp.where(positions == (picked + 1) % tile_total, lowest, flat_counts)
    return flat_counts.astype(jnp.int32)


def level_of(stream_key, dims, cuts, least, top_value):
    factor_of, own = 1.0, jax.random.fold_in(stream_key, 6)
    for axis_at, parts in cuts:
        heights = jnp.exp(jax.random.uniform(jax.random.fold_in(own, axis_at), (parts,), jnp.float32, least / len(cuts), top_value / len(cuts)))
        factor_of = factor_of * jnp.repeat(heights, dims[axis_at] // parts).reshape([-1 if axis == axis_at else 1 for axis in range(len(dims))])
    return factor_of


def gaussian(rng, dims, spread, bound, pieces=(), kind=jnp.bfloat16):
    factor_of = level_of(rng, dims, pieces, -0.22, 0.18) if pieces else 1.0
    result = jax.random.normal(rng, dims, jnp.float32) * spread * factor_of
    return jnp.minimum(jnp.maximum(result, -bound), bound).astype(kind)


def setup_inputs(seed: int = 0) -> dict:
    key_list = jax.random.split(jax.random.key(seed), 10)
    coords = gaussian(key_list[0], (REPLICAS, BLOCKS, 3, 128), 1.0, 6.0, ((0, 8), (1, 16)), jnp.float32)
    atom_weight = jnp.clip(jnp.exp(math.log(0.05) - 2.3025851 * jax.random.uniform(key_list[1], (BLOCKS, 128), jnp.float32) ** level_of(key_list[1], (BLOCKS, 128), ((0, 16),), -0.2, 0.2)), 0.005, 0.05)
    centers = gaussian(key_list[2], (TILES, 3, 128), 1.0, 6.0, ((0, 16),), jnp.float32)
    inv_width = jnp.clip(jnp.exp(math.log(0.5) - 1.609438 * jax.random.uniform(key_list[3], (TILES, 128), jnp.float32) ** level_of(key_list[3], (TILES, 128), ((0, 16),), -0.2, 0.2)), 0.1, 0.5)
    density = jnp.clip(4.0 * jax.random.uniform(key_list[4], (TILES, 128), jnp.float32) ** level_of(key_list[4], (TILES, 128), ((0, 16),), -0.2, 0.2), 0.0, 4.0)
    variance = jnp.clip(jnp.exp(math.log(4.0) - 1.3862944 * jax.random.uniform(key_list[5], (TILES, 128), jnp.float32) ** level_of(key_list[5], (TILES, 128), ((0, 16),), -0.2, 0.2)), 1.0, 4.0)
    tile_blocks = draw_tile_blocks(jax.random.fold_in(key_list[9], 71), 0)
    tile_counts = draw_tile_counts(jax.random.fold_in(key_list[9], 71), 0)
    send_blocks = draw_send_blocks(jax.random.fold_in(key_list[9], 71), 0)
    return {"coords": coords, "atom_weight": atom_weight, "centers": centers, "inv_width": inv_width, "density": density, "variance": variance, "tile_blocks": tile_blocks, "tile_counts": tile_counts, "send_blocks": send_blocks}


def gaussian_kernel(block_coords, centre, width_rate):
    offset_c = block_coords[None, :, 0, :] - centre[0][:, None, None]
    dist_sq = offset_c * offset_c
    for component in (1, 2):
        offset_c = block_coords[None, :, component, :] - centre[component][:, None, None]
        dist_sq = dist_sq + offset_c * offset_c
    return jnp.exp(-width_rate[:, None, None] * dist_sq)


def model_intersection(block_coords, block_weight, centre, width_rate):
    kernel = gaussian_kernel(block_coords, centre, width_rate)
    return jnp.einsum("gja,ja->g", kernel, block_weight, precision=lax.Precision.HIGHEST)


def restraint_pull(block_coords, block_weight, centre, width_rate, pull_rate):
    kernel = gaussian_kernel(block_coords, centre, width_rate)
    weighted = jnp.einsum("gja,g->ja", kernel, pull_rate, precision=lax.Precision.HIGHEST)
    shifted = jnp.einsum("gja,cg->jca", kernel, pull_rate[None, :] * centre, precision=lax.Precision.HIGHEST)
    return 2.0 * block_weight[:, None, :] * (block_coords * weighted[:, None, :] - shifted)


def reference(coords, atom_weight, centers, inv_width, density, variance, tile_blocks, tile_counts, send_blocks):
    slot_count = N_SP * CAP
    sources = jnp.arange(N_SP, dtype=jnp.int32)
    slot_global = jnp.transpose(sources[:, None, None] * BLK_DEV + send_blocks, (1, 0, 2)).reshape(N_SP, slot_count)
    own_global = sources[:, None] * BLK_DEV + jnp.arange(BLK_DEV, dtype=jnp.int32)[None, :]
    table_global = jnp.concatenate([own_global.astype(jnp.int32), slot_global.astype(jnp.int32)], axis=1)
    owners = jnp.arange(TILES, dtype=jnp.int32) // TILE_DEV
    block_ids = jnp.take_along_axis(table_global[owners], tile_blocks, axis=1).astype(jnp.int32)
    live = (jnp.arange(MAXB, dtype=jnp.int32)[None, :] < tile_counts[:, None]).astype(jnp.float32)
    bunch_size = 16
    round_count = TILES // bunch_size
    replica_count = coords.shape[0]

    def slices(which):
        start = (which * bunch_size).astype(jnp.int32)
        ids_here = lax.dynamic_slice_in_dim(block_ids, start, bunch_size, 0)
        live_here = lax.dynamic_slice_in_dim(live, start, bunch_size, 0)
        centre_here = lax.dynamic_slice_in_dim(centers, start, bunch_size, 0)
        rate_here = lax.dynamic_slice_in_dim(inv_width, start, bunch_size, 0)
        block_coords = coords[:, ids_here]
        block_weight = atom_weight[ids_here] * live_here[:, :, None]
        return start, block_coords, block_weight, centre_here, rate_here

    def first_pass(which):
        start, block_coords, block_weight, centre_here, rate_here = slices(which)
        per_tile = jax.vmap(model_intersection)
        return jax.vmap(per_tile, (0, None, None, None))(block_coords, block_weight, centre_here, rate_here)

    rounds = jnp.arange(round_count, dtype=jnp.int32)
    model = lax.map(first_pass, rounds)
    model = jnp.transpose(model, (1, 0, 2, 3)).reshape(replica_count, TILES, 128)
    mean_model = jnp.sum(model, axis=0) / N_REP
    pull_rate = (mean_model - density) / variance * inv_width

    def second_pass(which):
        start, block_coords, block_weight, centre_here, rate_here = slices(which)
        pull_here = lax.dynamic_slice_in_dim(pull_rate, start, bunch_size, 0)
        per_tile = jax.vmap(restraint_pull)
        return jax.vmap(per_tile, (0, None, None, None, None))(block_coords, block_weight, centre_here, rate_here, pull_here)

    pulls = lax.map(second_pass, rounds)
    pulls = jnp.transpose(pulls, (1, 0, 2, 3, 4, 5)).reshape(replica_count, TILES * MAXB, 3, 128)
    flat_ids = block_ids.reshape(-1)

    def gather_forces(replica_pulls):
        return jax.ops.segment_sum(replica_pulls, flat_ids, num_segments=BLOCKS)

    forces = jax.vmap(gather_forces)(pulls)
    return forces, mean_model
```

```python
import functools

import jax
import jax.numpy as jnp
from jax import lax
from jax.experimental import pallas as pl
from jax.experimental.pallas import tpu as pltpu
from jax.sharding import PartitionSpec as P

MESH = pl.DeviceIdType.MESH
BF = jnp.bfloat16
F32 = jnp.float32
I32 = jnp.int32
VMEM = pl.BlockSpec(memory_space=pltpu.VMEM)
SMEM = pl.BlockSpec(memory_space=pltpu.SMEM)

OFFSETS = (1, 2, 3, 8, 13, 14, 15)
CAP = 16
OWN = 512
HALO = len(OFFSETS) * CAP
TABLE = OWN + HALO
DUMMY = TABLE
ROWS = TABLE + CAP
TILES = 32
LIST = 32
STEPS = TILES * LIST // 2
FLAT = STEPS + 64
DEPTH = 48
LOG2E = 1.4426950408889634


def params(limit_mib, collective_id=None):
    more = {} if collective_id is None else {"collective_id": collective_id, "has_side_effects": True}
    return pltpu.CompilerParams(vmem_limit_bytes=limit_mib << 20, **more)


def sp_peer(offset):
    return (lax.axis_index("rep"), lax.rem(lax.axis_index("sp") + offset, 16))


def greet(peers):
    barrier = pltpu.get_barrier_semaphore()
    for peer in peers:
        pl.semaphore_signal(barrier, inc=1, device_id=peer, device_id_type=MESH)
    pl.semaphore_wait(barrier, len(peers))


def halo_kernel(send_ref, coords_ref, weight_ref, out_ref, pack, send_sem, recv_sem):
    me = lax.axis_index("sp")
    greet([sp_peer(o) for o in OFFSETS])
    copies = []
    for p, offset in enumerate(OFFSETS):
        to = lax.rem(me + 16 - offset, 16)
        for k in range(CAP):
            b = send_ref[to, k]
            pack[p * CAP + k, 0:3, :] = coords_ref[b]
            pack[p * CAP + k, 3:4, :] = weight_ref[pl.ds(b, 1), :]
        copy = pltpu.make_async_remote_copy(
            src_ref=pack.at[pl.ds(p * CAP, CAP)],
            dst_ref=out_ref.at[pl.ds(p * CAP, CAP)],
            send_sem=send_sem.at[p],
            recv_sem=recv_sem.at[p],
            device_id=(lax.axis_index("rep"), to),
            device_id_type=MESH,
        )
        copy.start()
        copies.append(copy)
    for copy in copies:
        copy.wait()


def halo(send, coords, weight):
    return pl.pallas_call(
        halo_kernel,
        out_shape=jax.ShapeDtypeStruct((HALO, 4, 128), F32),
        in_specs=[SMEM, VMEM, VMEM],
        out_specs=VMEM,
        scratch_shapes=[
            pltpu.VMEM((HALO, 4, 128), F32),
            pltpu.SemaphoreType.DMA((len(OFFSETS),)),
            pltpu.SemaphoreType.DMA((len(OFFSETS),)),
        ],
        compiler_params=params(16, 0),
        name="halo",
    )(send, coords, weight)


def pieces(x):
    hi = x.astype(BF).astype(F32)
    rest = x - hi
    mid = rest.astype(BF).astype(F32)
    return hi, mid, rest - mid


def features(xyz):
    square = jnp.sum(xyz * xyz, axis=0, keepdims=True)
    hi, mid, lo = pieces(jnp.concatenate([xyz, square], axis=0))
    return jnp.concatenate([hi, mid, hi, lo], axis=0).astype(BF)


def tile_rates(centers, rate):
    slope = rate * LOG2E
    rows = jnp.concatenate([2.0 * slope * centers, -slope], axis=0)
    hi, mid, lo = pieces(rows)
    size = jnp.sum(centers * centers, axis=0, keepdims=True)
    c_hi, c_mid, c_lo = pieces(-slope * size)
    zero8 = jnp.zeros((8, 128), F32)
    zero13 = jnp.zeros((13, 128), F32)
    return jnp.concatenate([hi, hi, mid, hi, lo, mid, zero8, c_hi, c_mid, c_lo, zero13], axis=0)


def unpack(word):
    return lax.shift_right_logical(word, 20), lax.shift_right_logical(word, 10) & 1023, word & 1023


def exponents(flat, rates, feats, at, out_ref, slot):
    t, b1, b2 = unpack(flat[at])
    pair = jnp.concatenate([feats[b1], feats[b2]], axis=1)
    ones = jnp.ones((16, 256), BF)
    out_ref[slot] = jnp.dot(
        rates[t], jnp.concatenate([pair, pair, ones], axis=0), preferred_element_type=F32
    )


def model_kernel(
    turns, depth, count, flat, coords, weight, received, centers, width,
    model_ref, rates, feats, weights, power, total,
):
    def own(b, carry):
        feats[b] = features(coords[b])
        return carry

    lax.fori_loop(0, OWN, own, 0, unroll=8)

    def slot(b, carry):
        feats[OWN + b] = features(received[b, 0:3, :])
        weights[pl.ds(OWN + b, 1), :] = received[b, 3:4, :]
        return carry

    lax.fori_loop(0, HALO, slot, 0, unroll=8)
    weights[0:OWN, :] = weight[...]
    for b in range(TABLE, ROWS):
        feats[b] = jnp.zeros((16, 128), BF)
    weights[TABLE:ROWS, :] = jnp.zeros((ROWS - TABLE, 128), F32)

    def tile(t, carry):
        rows = tile_rates(centers[t], width[pl.ds(t, 1), :])
        rates[t] = jnp.transpose(rows).astype(BF)
        total[t] = jnp.zeros((128, 128), F32)
        return carry

    lax.fori_loop(0, TILES, tile, 0, unroll=2)

    def add(at, src):
        t, b1, b2 = unpack(flat[at])
        k = jnp.exp2(power[src])
        total[t] += k[:, :128] * weights[pl.ds(b1, 1), :] + k[:, 128:] * weights[pl.ds(b2, 1), :]

    for d in range(depth):
        exponents(flat, rates, feats, d, power, d)

    def body(i, carry):
        first = turns * i
        for u in range(turns):
            exponents(flat, rates, feats, first + u + depth, power, (u + depth) % turns)
            add(first + u, u)
        return carry

    lax.fori_loop(0, (count[0] + turns - 1) // turns, body, 0)
    for t in range(TILES):
        model_ref[t, :] = jnp.sum(total[t], axis=-1)


def model_pass(count, flat, coords, weight, received, centers, width):
    turns, depth = 16, 4
    return pl.pallas_call(
        functools.partial(model_kernel, turns, depth),
        out_shape=(
            jax.ShapeDtypeStruct((TILES, 128), F32),
            jax.ShapeDtypeStruct((TILES, 128, DEPTH), BF),
            jax.ShapeDtypeStruct((ROWS, 16, 128), BF),
        ),
        in_specs=[SMEM, SMEM, VMEM, VMEM, VMEM, VMEM, VMEM],
        out_specs=(VMEM, VMEM, VMEM),
        scratch_shapes=[
            pltpu.VMEM((ROWS, 128), F32),
            pltpu.VMEM((turns, 128, 256), F32),
            pltpu.VMEM((TILES, 128, 128), F32),
        ],
        compiler_params=params(40),
        name="model_pass",
    )(count, flat, coords, weight, received, centers, width)


def replica_kernel(
    model, centers, width, density, variance, mean_ref, pull_ref, slots, send_sem, recv_sem
):
    rep, sp = lax.axis_index("rep"), lax.axis_index("sp")
    greet([(lax.rem(rep + d, 8), sp) for d in range(1, 8)])
    copies = []
    for d in range(1, 8):
        copy = pltpu.make_async_remote_copy(
            src_ref=model,
            dst_ref=slots.at[rep],
            send_sem=send_sem.at[d],
            recv_sem=recv_sem.at[d],
            device_id=(lax.rem(rep + d, 8), sp),
            device_id_type=MESH,
        )
        copy.start()
        copies.append(copy)
    slots[rep] = model[...]
    for copy in copies:
        copy.wait()
    sum_ = slots[0]
    for r in range(1, 8):
        sum_ = sum_ + slots[r]
    mean = sum_ * 0.125
    mean_ref[...] = mean
    rate = (mean - density[...]) / variance[...] * width[...]
    for t in range(TILES):
        row = rate[t : t + 1, :]
        four = jnp.concatenate([row, row * centers[t]], axis=0)
        hi = four.astype(BF).astype(F32)
        rows = jnp.concatenate([hi, four - hi, jnp.zeros((8, 128), F32)], axis=0).astype(BF)
        pull_ref[t] = jnp.concatenate([rows, rows], axis=1)


def replica_sum(model, centers, width, density, variance):
    return pl.pallas_call(
        replica_kernel,
        out_shape=(
            jax.ShapeDtypeStruct((TILES, 128), F32),
            jax.ShapeDtypeStruct((TILES, 16, 256), BF),
        ),
        in_specs=[VMEM] * 5,
        out_specs=(VMEM, VMEM),
        scratch_shapes=[
            pltpu.VMEM((8, TILES, 128), F32),
            pltpu.SemaphoreType.DMA((8,)),
            pltpu.SemaphoreType.DMA((8,)),
        ],
        compiler_params=params(16, 1),
        name="replica_sum",
    )(model, centers, width, density, variance)


def force_kernel(
    turns, depth, count, flat, rates, feats, pulls, coords, weight, received,
    own_ref, slot_ref, moments, power, split,
):
    def clear(b, carry):
        moments[b] = jnp.zeros((8, 128), F32)
        return carry

    lax.fori_loop(0, ROWS, clear, 0, unroll=8)

    def raise_(src):
        k = jnp.exp2(power[src])
        hi = k.astype(BF)
        split[src, :128] = hi
        split[src, 128:] = (k - hi.astype(F32)).astype(BF)

    def reduce(at, src):
        t, b1, b2 = unpack(flat[at])
        both = jnp.dot(pulls[t], split[src], preferred_element_type=F32)
        moments[b1] += both[:8, :128]
        moments[b2] += both[:8, 128:]

    for d in range(2 * depth):
        exponents(flat, rates, feats, d, power, d)
    for d in range(depth):
        raise_(d)

    def body(i, carry):
        first = turns * i
        for u in range(turns):
            exponents(flat, rates, feats, first + u + 2 * depth, power, (u + 2 * depth) % turns)
            raise_((u + depth) % turns)
            reduce(first + u, u)
        return carry

    lax.fori_loop(0, (count[0] + turns - 1) // turns, body, 0)

    def pull(eight, xyz, weights):
        four = eight[0:4] + eight[4:8]
        return 2.0 * weights * (xyz * four[0:1] - four[1:4])

    def own(b, carry):
        own_ref[b] = pull(moments[b], coords[b], weight[pl.ds(b, 1), :])
        return carry

    lax.fori_loop(0, OWN, own, 0, unroll=8)

    def slot(b, carry):
        got = received[b]
        slot_ref[b, 0:3, :] = pull(moments[OWN + b], got[0:3], got[3:4])
        return carry

    lax.fori_loop(0, HALO, slot, 0, unroll=8)


def force_pass(count, flat, rates, feats, pulls, coords, weight, received):
    turns, depth = 16, 2
    return pl.pallas_call(
        functools.partial(force_kernel, turns, depth),
        out_shape=(
            jax.ShapeDtypeStruct((OWN, 3, 128), F32),
            jax.ShapeDtypeStruct((HALO, 4, 128), F32),
        ),
        in_specs=[SMEM, SMEM] + [VMEM] * 6,
        out_specs=(VMEM, VMEM),
        scratch_shapes=[
            pltpu.VMEM((ROWS, 8, 128), F32),
            pltpu.VMEM((turns, 128, 256), F32),
            pltpu.VMEM((turns, 256, 256), BF),
        ],
        compiler_params=params(40),
        name="force_pass",
    )(count, flat, rates, feats, pulls, coords, weight, received)


def return_kernel(slot_ref, out_ref, send_sem, recv_sem):
    greet([sp_peer(o) for o in OFFSETS])
    copies = []
    for p, offset in enumerate(OFFSETS):
        copy = pltpu.make_async_remote_copy(
            src_ref=slot_ref.at[pl.ds(p * CAP, CAP)],
            dst_ref=out_ref.at[pl.ds(p * CAP, CAP)],
            send_sem=send_sem.at[p],
            recv_sem=recv_sem.at[p],
            device_id=sp_peer(offset),
            device_id_type=MESH,
        )
        copy.start()
        copies.append(copy)
    for copy in copies:
        copy.wait()


def return_forces(slots):
    return pl.pallas_call(
        return_kernel,
        out_shape=jax.ShapeDtypeStruct((HALO, 4, 128), F32),
        in_specs=[VMEM],
        out_specs=VMEM,
        scratch_shapes=[
            pltpu.SemaphoreType.DMA((len(OFFSETS),)),
            pltpu.SemaphoreType.DMA((len(OFFSETS),)),
        ],
        compiler_params=params(16, 2),
        name="return_forces",
    )(slots)


def merge_kernel(send_ref, own_ref, back_ref, out_ref):
    out_ref[...] = own_ref[...]
    me = lax.axis_index("sp")
    for p, offset in enumerate(OFFSETS):
        to = lax.rem(me + 16 - offset, 16)
        for k in range(CAP):
            b = send_ref[to, k]
            out_ref[b] += back_ref[p * CAP + k, 0:3, :]


def merge(send, own, back):
    return pl.pallas_call(
        merge_kernel,
        out_shape=jax.ShapeDtypeStruct((OWN, 3, 128), F32),
        in_specs=[SMEM, VMEM, VMEM],
        out_specs=VMEM,
        compiler_params=params(16),
        name="merge",
    )(send, own, back)


def flat_list(tile_blocks, tile_counts):
    me = lax.axis_index("sp")
    slot = tile_blocks - OWN
    offset = (slot // CAP - me) & 15
    place = jnp.where(offset < 4, offset - 1, jnp.where(offset == 8, 3, offset - 9))
    ids = jnp.where(slot < 0, tile_blocks, OWN + place * CAP + (slot & (CAP - 1)))
    ids = jnp.where(jnp.arange(LIST, dtype=I32)[None, :] < tile_counts[:, None], ids, DUMMY)
    ids = ids.reshape(TILES, LIST // 2, 2)
    words = (jnp.arange(TILES, dtype=I32)[:, None] << 20) | (ids[:, :, 0] << 10) | ids[:, :, 1]
    steps = (tile_counts + 1) >> 1
    earlier = jnp.arange(TILES, dtype=I32)[None, :] < jnp.arange(TILES, dtype=I32)[:, None]
    base = jnp.sum(jnp.where(earlier, steps[None, :], 0), axis=1)
    at = jnp.arange(LIST // 2, dtype=I32)[None, :]
    place = jnp.where(at < steps[:, None], base[:, None] + at, -1).reshape(STEPS)
    hit = place[None, :] == jnp.arange(FLAT, dtype=I32)[:, None]
    count = jnp.sum(steps)
    flat = jnp.sum(jnp.where(hit, words.reshape(STEPS)[None, :], 0), axis=1)
    flat = jnp.where(jnp.arange(FLAT, dtype=I32) < count, flat, (DUMMY << 10) | DUMMY)
    return count[None], flat


def local(
    coords, atom_weight, centers, inv_width, density, variance, tile_blocks, tile_counts, send_blocks
):
    own, send = coords[0], send_blocks[0]
    received = halo(send, own, atom_weight)
    count, flat = flat_list(tile_blocks, tile_counts)
    model, rates, feats = model_pass(count, flat, own, atom_weight, received, centers, inv_width)
    mean, pulls = replica_sum(model, centers, inv_width, density, variance)
    forces, slots = force_pass(count, flat, rates, feats, pulls, own, atom_weight, received)
    back = return_forces(slots)
    return merge(send, forces, back)[None], mean


def solution(mesh):
    return jax.shard_map(
        local,
        mesh=mesh,
        in_specs=(
            P("rep", "sp", None, None),
            P("sp", None),
            P("sp", None, None),
            P("sp", None),
            P("sp", None),
            P("sp", None),
            P("sp", None),
            P("sp"),
            P("sp", None, None),
        ),
        out_specs=(P("rep", "sp", None, None), P("sp", None)),
        check_vma=False,
    )
```

```python
import functools

import jax
import jax.numpy as jnp
from jax import lax
from jax.experimental import pallas as pl
from jax.experimental.pallas import tpu as pltpu
from jax.sharding import PartitionSpec as P

MESH = pl.DeviceIdType.MESH
BF = jnp.bfloat16
F32 = jnp.float32
I32 = jnp.int32
VMEM = pl.BlockSpec(memory_space=pltpu.VMEM)
SMEM = pl.BlockSpec(memory_space=pltpu.SMEM)

OFFSETS = (1, 2, 3, 8, 13, 14, 15)
CAP = 16
OWN = 512
HALO = len(OFFSETS) * CAP
TABLE = OWN + HALO
DUMMY = TABLE
ROWS = TABLE + CAP
TILES = 32
LIST = 32
STEPS = TILES * LIST // 2
FLAT = 640
SAVED = 320
BACK = 3 * CAP
DEPTH = 48
WORK = 32
RING = 8
LOG2E = 1.4426950408889634


def params(limit_mib, collective_id=None):
    more = {} if collective_id is None else {"collective_id": collective_id, "has_side_effects": True}
    return pltpu.CompilerParams(vmem_limit_bytes=limit_mib << 20, **more)


def sp_peer(offset):
    return (lax.axis_index("rep"), lax.rem(lax.axis_index("sp") + offset, 16))


def greet(peers):
    barrier = pltpu.get_barrier_semaphore()
    for peer in peers:
        pl.semaphore_signal(barrier, inc=1, device_id=peer, device_id_type=MESH)
    pl.semaphore_wait(barrier, len(peers))


def pieces(x):
    hi = x.astype(BF).astype(F32)
    rest = x - hi
    mid = rest.astype(BF).astype(F32)
    return hi, mid, rest - mid


def put_features(xyz, feats, first, lines, at):
    square = xyz[0] * xyz[0] + xyz[1] * xyz[1] + xyz[2] * xyz[2]
    for row, value in enumerate((*xyz, square)):
        hi, mid, lo = pieces(value)
        for group, piece in enumerate((hi, mid, hi, lo)):
            lines[pl.ds(at * 128 + 4 * group + row, 8, stride=16), :] = piece
    for b in range(8):
        feats[first + b] = lines[at * 128 + 16 * b : at * 128 + 16 * b + 16, :].astype(BF)


def put_rates(centers, width, rates, lines):
    slope = width[...] * LOG2E
    x = [centers[c] for c in range(3)]
    size = x[0] * x[0] + x[1] * x[1] + x[2] * x[2]
    zero = jnp.zeros((TILES, 128), F32)
    rows = [zero] * DEPTH
    for c, value in enumerate([2.0 * slope * x[0], 2.0 * slope * x[1], 2.0 * slope * x[2], -slope]):
        hi, mid, lo = pieces(value)
        for group, piece in enumerate((hi, hi, mid, hi, lo, mid)):
            rows[4 * group + c] = piece
    for at, piece in enumerate(pieces(-slope * size)):
        rows[32 + at] = piece
    for r in range(DEPTH):
        for q in range(TILES // 8):
            lines[pl.ds(8 * q * DEPTH + r, 8, stride=DEPTH), :] = rows[r][8 * q : 8 * q + 8]

    def tile(t, carry):
        block = lines[pl.ds(pl.multiple_of(t * DEPTH, 8), DEPTH), :]
        rates[t] = jnp.transpose(block).astype(BF)
        return carry

    lax.fori_loop(0, TILES, tile, 0, unroll=4)


def flat_list(lists, counts, flat):
    me = lax.axis_index("sp")
    ids = lists[...]
    slot = ids - OWN
    offset = (lax.shift_right_arithmetic(slot, 4) - me) & 15
    place = jnp.where(offset < 4, offset - 1, jnp.where(offset == 8, 3, offset - 9))
    ids = jnp.where(slot < 0, ids, OWN + place * CAP + (slot & (CAP - 1))).astype(F32)
    row = jnp.broadcast_to(counts[...], (TILES, TILES))
    sub = lax.broadcasted_iota(I32, (TILES, TILES), 0)
    lane = lax.broadcasted_iota(I32, (TILES, TILES), 1)
    steps_row = lax.shift_right_logical(row + 1, 1)
    count = jnp.sum(jnp.where(lane == sub, row, 0).astype(F32), axis=1, keepdims=True)
    steps = jnp.sum(jnp.where(lane == sub, steps_row, 0).astype(F32), axis=1, keepdims=True)
    base = jnp.sum(jnp.where(lane < sub, steps_row, 0).astype(F32), axis=1, keepdims=True)
    at = lax.broadcasted_iota(I32, (TILES, FLAT), 1).astype(F32)
    tile = lax.broadcasted_iota(I32, (TILES, FLAT), 0).astype(F32)
    hit = jnp.where((at >= base) & (at < base + steps), 1.0, 0.0)
    first = 2.0 * jnp.sum(hit * (at - base), axis=0, keepdims=True)
    which = jnp.sum(hit * tile, axis=0, keepdims=True)
    left = jnp.sum(hit * count, axis=0, keepdims=True)
    total = jnp.sum(steps, axis=0, keepdims=True)
    named = jnp.dot(
        jnp.transpose(ids), hit, preferred_element_type=F32, precision=lax.Precision.HIGHEST
    )
    one = jnp.sum(jnp.where(tile == first, named, 0.0), axis=0, keepdims=True)
    two = jnp.sum(jnp.where(tile == first + 1.0, named, 0.0), axis=0, keepdims=True)
    two = jnp.where(first + 1.0 < left, two, float(DUMMY))
    at = at[0:1]
    one = jnp.where(at < total, one, float(DUMMY))
    word = (which.astype(I32) << 20) | (one.astype(I32) << 10) | two.astype(I32)
    flat[...] = jnp.where(at == float(FLAT - 1), total.astype(I32), word)


def halo_kernel(
    send_ref, coords, weight, lists, counts, centers, width,
    received, feats, rates, weights, flat, pack, lines, send_sem, recv_sem,
):
    me = lax.axis_index("sp")
    greet([sp_peer(o) for o in OFFSETS])
    copies = []
    for p, offset in enumerate(OFFSETS):
        to = lax.rem(me + 16 - offset, 16)
        for k in range(CAP):
            b = send_ref[to, k]
            for c in range(3):
                pack[(p * 4 + c) * CAP + k : (p * 4 + c) * CAP + k + 1, :] = coords[c, pl.ds(b, 1), :]
            pack[(p * 4 + 3) * CAP + k : (p * 4 + 3) * CAP + k + 1, :] = weight[pl.ds(b, 1), :]
        copy = pltpu.make_async_remote_copy(
            src_ref=pack.at[pl.ds(p * 4 * CAP, 4 * CAP)],
            dst_ref=received.at[pl.ds(p * 4 * CAP, 4 * CAP)],
            send_sem=send_sem.at[p],
            recv_sem=recv_sem.at[p],
            device_id=(lax.axis_index("rep"), to),
            device_id_type=MESH,
        )
        copy.start()
        copies.append(copy)

    put_rates(centers, width, rates, lines)
    flat_list(lists, counts, flat)
    weights[0:OWN, :] = weight[...]
    weights[TABLE:ROWS, :] = jnp.zeros((ROWS - TABLE, 128), F32)
    for b in range(TABLE, ROWS):
        feats[b] = jnp.zeros((16, 128), BF)

    def own(i, carry):
        for u in range(4):
            b = pl.multiple_of(32 * i + 8 * u, 8)
            put_features([coords[c, pl.ds(b, 8), :] for c in range(3)], feats, b, lines, u)
        return carry

    lax.fori_loop(0, OWN // 32, own, 0)
    for p, copy in enumerate(copies):
        copy.wait()
        for h in range(CAP // 8):
            rows = [
                received[(p * 4 + c) * CAP + 8 * h : (p * 4 + c) * CAP + 8 * h + 8, :]
                for c in range(4)
            ]
            first = OWN + p * CAP + 8 * h
            put_features(rows[:3], feats, first, lines, (2 * p + h) % 4)
            weights[first : first + 8, :] = rows[3]


def halo(send, coords, weight, lists, counts, centers, width):
    return pl.pallas_call(
        halo_kernel,
        out_shape=(
            jax.ShapeDtypeStruct((4 * HALO, 128), F32),
            jax.ShapeDtypeStruct((ROWS, 16, 128), BF),
            jax.ShapeDtypeStruct((TILES, 128, DEPTH), BF),
            jax.ShapeDtypeStruct((ROWS, 128), F32),
            jax.ShapeDtypeStruct((1, FLAT), I32),
        ),
        in_specs=[SMEM] + [VMEM] * 6,
        out_specs=(VMEM,) * 5,
        scratch_shapes=[
            pltpu.VMEM((4 * HALO, 128), F32),
            pltpu.VMEM((TILES * DEPTH, 128), F32),
            pltpu.SemaphoreType.DMA((len(OFFSETS),)),
            pltpu.SemaphoreType.DMA((len(OFFSETS),)),
        ],
        compiler_params=params(4, 0),
        name="halo",
    )(send, coords, weight, lists, counts, centers, width)


def unpack(word):
    return lax.shift_right_logical(word, 20), lax.shift_right_logical(word, 10) & 1023, word & 1023


def exponents(flat, rates, feats, at):
    t, b1, b2 = unpack(flat[0, at])
    pair = jnp.concatenate([feats[b1], feats[b2]], axis=1)
    ones = jnp.ones((16, 256), BF)
    return jnp.dot(
        rates[t], jnp.concatenate([pair, pair, ones], axis=0), preferred_element_type=F32
    )


def turns_of(count, turns):
    return lax.div(count + (turns - 1), turns)


def model_kernel(turns, depth, flat, rates, feats, weights, model, power, total):
    count = flat[0, FLAT - 1]
    for t in range(TILES):
        total[t] = jnp.zeros((128, 128), F32)

    def add(at, k):
        t, b1, b2 = unpack(flat[0, at])
        total[t] += k[:, :128] * weights[pl.ds(b1, 1), :] + k[:, 128:] * weights[pl.ds(b2, 1), :]

    for d in range(depth):
        power[d] = exponents(flat, rates, feats, d)

    def body(i, carry):
        first = turns * i
        for u in range(turns):
            power[first + u + depth] = exponents(flat, rates, feats, first + u + depth)
            add(first + u, jnp.exp2(power[first + u]))
        return carry

    lax.fori_loop(0, turns_of(jnp.minimum(count, SAVED), turns), body, 0)

    def rest(i, carry):
        for u in range(8):
            at = SAVED + 8 * i + u
            add(at, jnp.exp2(exponents(flat, rates, feats, at)))
        return carry

    lax.fori_loop(0, turns_of(jnp.maximum(count - SAVED, 0), 8), rest, 0)
    for t in range(TILES):
        model[t, :] = jnp.sum(total[t], axis=-1)


def model_pass(flat, rates, feats, weights):
    turns, depth = WORK, 4
    return pl.pallas_call(
        functools.partial(model_kernel, turns, depth),
        out_shape=(
            jax.ShapeDtypeStruct((TILES, 128), F32),
            jax.ShapeDtypeStruct((SAVED + depth, 128, 256), F32),
        ),
        in_specs=[SMEM, VMEM, VMEM, VMEM],
        out_specs=(VMEM, VMEM),
        scratch_shapes=[pltpu.VMEM((TILES, 128, 128), F32)],
        compiler_params=params(4),
        name="model_pass",
    )(flat, rates, feats, weights)


def replica_kernel(
    model, centers, width, density, variance, mean_ref, pull_ref, slots, lines, send_sem, recv_sem
):
    rep, sp = lax.axis_index("rep"), lax.axis_index("sp")
    greet([(lax.rem(rep + d, 8), sp) for d in range(1, 8)])
    copies = []
    for d in range(1, 8):
        copy = pltpu.make_async_remote_copy(
            src_ref=model,
            dst_ref=slots.at[rep],
            send_sem=send_sem.at[d],
            recv_sem=recv_sem.at[d],
            device_id=(lax.rem(rep + d, 8), sp),
            device_id_type=MESH,
        )
        copy.start()
        copies.append(copy)
    slots[rep] = model[...]
    lines[...] = jnp.zeros((TILES * 16, 128), F32)
    for copy in copies:
        copy.wait()
    sum_ = slots[0]
    for r in range(1, 8):
        sum_ = sum_ + slots[r]
    mean = sum_ * 0.125
    mean_ref[...] = mean
    rate = (mean - density[...]) / variance[...] * width[...]
    for row, value in enumerate([rate] + [rate * centers[c] for c in range(3)]):
        hi = value.astype(BF).astype(F32)
        for q in range(TILES // 8):
            lines[pl.ds(128 * q + row, 8, stride=16), :] = hi[8 * q : 8 * q + 8]
            lines[pl.ds(128 * q + 4 + row, 8, stride=16), :] = (value - hi)[8 * q : 8 * q + 8]
    for t in range(TILES):
        rows = lines[16 * t : 16 * t + 16, :].astype(BF)
        pull_ref[t] = jnp.concatenate([rows, rows], axis=1)


def replica_sum(model, centers, width, density, variance):
    return pl.pallas_call(
        replica_kernel,
        out_shape=(
            jax.ShapeDtypeStruct((TILES, 128), F32),
            jax.ShapeDtypeStruct((TILES, 16, 256), BF),
        ),
        in_specs=[VMEM] * 5,
        out_specs=(VMEM, VMEM),
        scratch_shapes=[
            pltpu.VMEM((8, TILES, 128), F32),
            pltpu.VMEM((TILES * 16, 128), F32),
            pltpu.SemaphoreType.DMA((8,)),
            pltpu.SemaphoreType.DMA((8,)),
        ],
        compiler_params=params(4, 1),
        name="replica_sum",
    )(model, centers, width, density, variance)


def force_kernel(
    turns, depth, flat, power, rates, feats, pulls, coords, weights, received,
    own_ref, slot_ref, moments, split,
):
    count = flat[0, FLAT - 1]

    def clear(i, carry):
        moments[pl.ds(pl.multiple_of(128 * i, 128), 128), :] = jnp.zeros((128, 128), F32)
        return carry

    lax.fori_loop(0, ROWS // 16, clear, 0)

    def raise_(value, src):
        k = jnp.exp2(value)
        hi = k.astype(BF)
        split[src, :128] = hi
        split[src, 128:] = (k - hi.astype(F32)).astype(BF)

    def reduce(at, src):
        t, b1, b2 = unpack(flat[0, at])
        both = jnp.dot(pulls[t], split[src], preferred_element_type=F32)
        moments[pl.ds(pl.multiple_of(8 * b1, 8), 8), :] += both[:8, :128]
        moments[pl.ds(pl.multiple_of(8 * b2, 8), 8), :] += both[:8, 128:]

    for d in range(depth):
        raise_(power[d], d)

    def body(i, carry):
        first = turns * i
        for u in range(turns):
            raise_(power[first + u + depth], (u + depth) % RING)
            reduce(first + u, u % RING)
        return carry

    lax.fori_loop(0, turns_of(jnp.minimum(count, SAVED), turns), body, 0)

    def rest(i, carry):
        for u in range(8):
            at = SAVED + 8 * i + u
            raise_(exponents(flat, rates, feats, at), u)
            reduce(at, u)
        return carry

    lax.fori_loop(0, turns_of(jnp.maximum(count - SAVED, 0), 8), rest, 0)

    def summed(first):
        return [
            moments[pl.ds(8 * first + c, 8, stride=8), :]
            + moments[pl.ds(8 * first + 4 + c, 8, stride=8), :]
            for c in range(4)
        ]

    def own(i, carry):
        for u in range(4):
            b = pl.multiple_of(32 * i + 8 * u, 8)
            four = summed(b)
            twice = 2.0 * weights[pl.ds(b, 8), :]
            for c in range(3):
                own_ref[c, pl.ds(b, 8), :] = twice * (coords[c, pl.ds(b, 8), :] * four[0] - four[1 + c])
        return carry

    lax.fori_loop(0, OWN // 32, own, 0)
    for p in range(len(OFFSETS)):
        for h in range(CAP // 8):
            four = summed(OWN + p * CAP + 8 * h)
            at = p * 4 * CAP + 8 * h
            twice = 2.0 * received[at + 3 * CAP : at + 3 * CAP + 8, :]
            for c in range(3):
                xyz = received[at + c * CAP : at + c * CAP + 8, :]
                to = p * BACK + c * CAP + 8 * h
                slot_ref[to : to + 8, :] = twice * (xyz * four[0] - four[1 + c])


def force_pass(flat, power, rates, feats, pulls, coords, weights, received):
    turns, depth = WORK, 2
    return pl.pallas_call(
        functools.partial(force_kernel, turns, depth),
        out_shape=(
            jax.ShapeDtypeStruct((3, OWN, 128), F32),
            jax.ShapeDtypeStruct((3 * HALO, 128), F32),
        ),
        in_specs=[SMEM] + [VMEM] * 7,
        out_specs=(VMEM, VMEM),
        scratch_shapes=[
            pltpu.VMEM((ROWS * 8, 128), F32),
            pltpu.VMEM((RING, 256, 256), BF),
        ],
        compiler_params=params(4),
        name="force_pass",
    )(flat, power, rates, feats, pulls, coords, weights, received)


def return_kernel(slot_ref, out_ref, send_sem, recv_sem):
    greet([sp_peer(o) for o in OFFSETS])
    copies = []
    for p, offset in enumerate(OFFSETS):
        copy = pltpu.make_async_remote_copy(
            src_ref=slot_ref.at[pl.ds(p * BACK, BACK)],
            dst_ref=out_ref.at[pl.ds(p * BACK, BACK)],
            send_sem=send_sem.at[p],
            recv_sem=recv_sem.at[p],
            device_id=sp_peer(offset),
            device_id_type=MESH,
        )
        copy.start()
        copies.append(copy)
    for copy in copies:
        copy.wait()


def return_forces(slots):
    return pl.pallas_call(
        return_kernel,
        out_shape=jax.ShapeDtypeStruct((3 * HALO, 128), F32),
        in_specs=[VMEM],
        out_specs=VMEM,
        scratch_shapes=[
            pltpu.SemaphoreType.DMA((len(OFFSETS),)),
            pltpu.SemaphoreType.DMA((len(OFFSETS),)),
        ],
        compiler_params=params(4, 2),
        name="return_forces",
    )(slots)


def merge_kernel(send_ref, own_ref, back_ref, out_ref):
    out_ref[...] = own_ref[...]
    me = lax.axis_index("sp")
    for p, offset in enumerate(OFFSETS):
        to = lax.rem(me + 16 - offset, 16)
        for k in range(CAP):
            b = send_ref[to, k]
            for c in range(3):
                row = p * BACK + c * CAP + k
                out_ref[c, pl.ds(b, 1), :] += back_ref[row : row + 1, :]


def merge(send, own, back):
    return pl.pallas_call(
        merge_kernel,
        out_shape=jax.ShapeDtypeStruct((3, OWN, 128), F32),
        in_specs=[SMEM, VMEM, VMEM],
        out_specs=VMEM,
        compiler_params=params(4),
        name="merge",
    )(send, own, back)


def local(
    coords, atom_weight, centers, inv_width, density, variance, tile_blocks, tile_counts, send_blocks
):
    own, send = jnp.transpose(coords[0], (1, 0, 2)), send_blocks[0]
    centers = jnp.transpose(centers, (1, 0, 2))
    received, feats, rates, weights, flat = halo(
        send, own, atom_weight, tile_blocks, tile_counts[None], centers, inv_width
    )
    model, power = model_pass(flat, rates, feats, weights)
    mean, pulls = replica_sum(model, centers, inv_width, density, variance)
    forces, slots = force_pass(flat, power, rates, feats, pulls, own, weights, received)
    back = return_forces(slots)
    return jnp.transpose(merge(send, forces, back), (1, 0, 2))[None], mean


def solution(mesh):
    return jax.shard_map(
        local,
        mesh=mesh,
        in_specs=(
            P("rep", "sp", None, None),
            P("sp", None),
            P("sp", None, None),
            P("sp", None),
            P("sp", None),
            P("sp", None),
            P("sp", None),
            P("sp"),
            P("sp", None, None),
        ),
        out_specs=(P("rep", "sp", None, None), P("sp", None)),
        check_vma=False,
    )
```

```python
import functools

import jax
import jax.numpy as jnp
from jax import lax
from jax.experimental import pallas as pl
from jax.experimental.pallas import tpu as pltpu
from jax.sharding import PartitionSpec as P

MESH = pl.DeviceIdType.MESH
BF = jnp.bfloat16
F32 = jnp.float32
I32 = jnp.int32
VMEM = pl.BlockSpec(memory_space=pltpu.VMEM)
SMEM = pl.BlockSpec(memory_space=pltpu.SMEM)
HBM = pl.BlockSpec(memory_space=pltpu.HBM)

OFFSETS = (1, 2, 3, 8, 13, 14, 15)
CAP = 16
OWN = 512
HALO = len(OFFSETS) * CAP
TABLE = OWN + HALO
DUMMY = TABLE
ROWS = TABLE + CAP
TILES = 32
LIST = 32
STEPS = TILES * LIST // 2
FLAT = 640
SURE = 10
FIXED = TILES * SURE
BACK = 3 * CAP
DEPTH = 48
RING = 8
GROUPS = 4
LOG2E = 1.4426950408889634


def params(limit_mib, collective_id=None):
    more = {} if collective_id is None else {"collective_id": collective_id, "has_side_effects": True}
    return pltpu.CompilerParams(vmem_limit_bytes=limit_mib << 20, **more)


def sp_peer(offset):
    return (lax.axis_index("rep"), lax.rem(lax.axis_index("sp") + offset, 16))


def greet(peers):
    barrier = pltpu.get_barrier_semaphore()
    for peer in peers:
        pl.semaphore_signal(barrier, inc=1, device_id=peer, device_id_type=MESH)
    pl.semaphore_wait(barrier, len(peers))


def pieces(x):
    hi = x.astype(BF).astype(F32)
    rest = x - hi
    mid = rest.astype(BF).astype(F32)
    return hi, mid, rest - mid


def put_features(xyz, feats, first, lines, at):
    square = xyz[0] * xyz[0] + xyz[1] * xyz[1] + xyz[2] * xyz[2]
    for row, value in enumerate((*xyz, square)):
        hi, mid, lo = pieces(value)
        for group, piece in enumerate((hi, mid, hi, lo)):
            lines[pl.ds(at * 128 + 4 * group + row, 8, stride=16), :] = piece
    for b in range(8):
        feats[first + b] = lines[at * 128 + 16 * b : at * 128 + 16 * b + 16, :].astype(BF)


def put_rates(centers, width, rates, lines):
    slope = width[...] * LOG2E
    x = [centers[c] for c in range(3)]
    size = x[0] * x[0] + x[1] * x[1] + x[2] * x[2]
    zero = jnp.zeros((TILES, 128), F32)
    rows = [zero] * DEPTH
    for c, value in enumerate([2.0 * slope * x[0], 2.0 * slope * x[1], 2.0 * slope * x[2], -slope]):
        hi, mid, lo = pieces(value)
        for group, piece in enumerate((hi, hi, mid, hi, lo, mid)):
            rows[4 * group + c] = piece
    for at, piece in enumerate(pieces(-slope * size)):
        rows[32 + at] = piece
    for r in range(DEPTH):
        for q in range(TILES // 8):
            lines[pl.ds(8 * q * DEPTH + r, 8, stride=DEPTH), :] = rows[r][8 * q : 8 * q + 8]

    def tile(t, carry):
        block = lines[pl.ds(pl.multiple_of(t * DEPTH, 8), DEPTH), :]
        rates[t] = jnp.transpose(block).astype(BF)
        return carry

    lax.fori_loop(0, TILES, tile, 0, unroll=4)


def flat_list(lists, counts, flat):
    me = lax.axis_index("sp")
    ids = lists[...]
    slot = ids - OWN
    offset = (lax.shift_right_arithmetic(slot, 4) - me) & 15
    place = jnp.where(offset < 4, offset - 1, jnp.where(offset == 8, 3, offset - 9))
    ids = jnp.where(slot < 0, ids, OWN + place * CAP + (slot & (CAP - 1))).astype(F32)
    row = jnp.broadcast_to(counts[...], (TILES, TILES))
    sub = lax.broadcasted_iota(I32, (TILES, TILES), 0)
    lane = lax.broadcasted_iota(I32, (TILES, TILES), 1)
    more_row = (lax.shift_right_logical(row + 1, 1) - SURE).astype(F32)
    count = jnp.sum(jnp.where(lane == sub, row.astype(F32), 0.0), axis=1, keepdims=True)
    more = jnp.sum(jnp.where(lane == sub, more_row, 0.0), axis=1, keepdims=True)
    base = jnp.sum(jnp.where(lane < sub, more_row, 0.0), axis=1, keepdims=True) + float(FIXED)
    at = lax.broadcasted_iota(I32, (TILES, FLAT), 1).astype(F32)
    tile = lax.broadcasted_iota(I32, (TILES, FLAT), 0).astype(F32)
    sure = (at >= SURE * tile) & (at < SURE * tile + SURE)
    hit = jnp.where(sure | ((at >= base) & (at < base + more)), 1.0, 0.0)
    step = jnp.where(sure, at - SURE * tile, at - base + SURE)
    first = 2.0 * jnp.sum(hit * step, axis=0, keepdims=True)
    which = jnp.sum(hit * tile, axis=0, keepdims=True)
    left = jnp.sum(hit * count, axis=0, keepdims=True)
    total = jnp.sum(more, axis=0, keepdims=True)
    named = jnp.dot(
        jnp.transpose(ids), hit, preferred_element_type=F32, precision=lax.Precision.HIGHEST
    )
    one = jnp.sum(jnp.where(tile == first, named, 0.0), axis=0, keepdims=True)
    two = jnp.sum(jnp.where(tile == first + 1.0, named, 0.0), axis=0, keepdims=True)
    two = jnp.where(first + 1.0 < left, two, float(DUMMY))
    at = at[0:1]
    one = jnp.where(at < total + float(FIXED), one, float(DUMMY))
    word = (which.astype(I32) << 20) | (one.astype(I32) << 10) | two.astype(I32)
    flat[...] = jnp.where(at == float(FLAT - 1), total.astype(I32), word)


def halo_kernel(
    send_hbm, coords_hbm, weight_hbm, lists_hbm, counts_hbm, centers_hbm, width_hbm, density_hbm, variance_hbm,
    received, feats, rates, weights, flat, coords, centers, width, density, variance,
    pack, lines, lists, counts, send_ref, near_sem, send_sem, recv_sem,
):
    me = lax.axis_index("sp")
    barrier = pltpu.get_barrier_semaphore()
    for offset in OFFSETS:
        pl.semaphore_signal(barrier, inc=1, device_id=sp_peer(offset), device_id_type=MESH)
    near = [
        pltpu.make_async_copy(src, dst, near_sem.at[i])
        for i, (src, dst) in enumerate((
            (send_hbm, send_ref),
            (coords_hbm, coords),
            (weight_hbm, weights.at[pl.ds(0, OWN)]),
            (centers_hbm, centers),
            (width_hbm, width),
            (lists_hbm, lists),
            (counts_hbm, counts),
            (density_hbm, density),
            (variance_hbm, variance),
        ))
    ]
    for copy in near:
        copy.start()
    for copy in near[:3]:
        copy.wait()

    def gather(p):
        to = lax.rem(me + 16 - OFFSETS[p], 16)
        for k in range(CAP):
            b = send_ref[to, k]
            for c in range(3):
                pack[(p * 4 + c) * CAP + k : (p * 4 + c) * CAP + k + 1, :] = coords[c, pl.ds(b, 1), :]
            pack[(p * 4 + 3) * CAP + k : (p * 4 + 3) * CAP + k + 1, :] = weights[pl.ds(b, 1), :]

    copies = []
    for p, offset in enumerate(OFFSETS):
        gather(p)
        if p == 0:
            pl.semaphore_wait(barrier, len(OFFSETS))
        copy = pltpu.make_async_remote_copy(
            src_ref=pack.at[pl.ds(p * 4 * CAP, 4 * CAP)],
            dst_ref=received.at[pl.ds(p * 4 * CAP, 4 * CAP)],
            send_sem=send_sem.at[p],
            recv_sem=recv_sem.at[p],
            device_id=sp_peer(16 - offset),
            device_id_type=MESH,
        )
        copy.start()
        copies.append(copy)

    for copy in near[3:]:
        copy.wait()
    put_rates(centers, width, rates, lines)
    flat_list(lists, counts, flat)
    weights[TABLE:ROWS, :] = jnp.zeros((ROWS - TABLE, 128), F32)
    for b in range(TABLE, ROWS):
        feats[b] = jnp.zeros((16, 128), BF)

    def own(i, carry):
        for u in range(4):
            b = pl.multiple_of(32 * i + 8 * u, 8)
            put_features([coords[c, pl.ds(b, 8), :] for c in range(3)], feats, b, lines, u)
        return carry

    lax.fori_loop(0, OWN // 32, own, 0)
    for p, copy in enumerate(copies):
        copy.wait()
        for h in range(CAP // 8):
            rows = [
                received[(p * 4 + c) * CAP + 8 * h : (p * 4 + c) * CAP + 8 * h + 8, :]
                for c in range(4)
            ]
            first = OWN + p * CAP + 8 * h
            put_features(rows[:3], feats, first, lines, (2 * p + h) % 4)
            weights[first : first + 8, :] = rows[3]


def halo(send, coords, weight, lists, counts, centers, width, density, variance):
    small = jax.ShapeDtypeStruct((TILES, 128), F32)
    return pl.pallas_call(
        halo_kernel,
        out_shape=(
            jax.ShapeDtypeStruct((4 * HALO, 128), F32),
            jax.ShapeDtypeStruct((ROWS, 16, 128), BF),
            jax.ShapeDtypeStruct((TILES, 128, DEPTH), BF),
            jax.ShapeDtypeStruct((ROWS, 128), F32),
            jax.ShapeDtypeStruct((1, FLAT), I32),
            jax.ShapeDtypeStruct((3, OWN, 128), F32),
            jax.ShapeDtypeStruct((3, TILES, 128), F32),
            small,
            small,
            small,
        ),
        in_specs=[HBM] * 9,
        out_specs=(VMEM,) * 10,
        scratch_shapes=[
            pltpu.VMEM((4 * HALO, 128), F32),
            pltpu.VMEM((TILES * DEPTH, 128), F32),
            pltpu.VMEM((TILES, LIST), I32),
            pltpu.VMEM((1, TILES), I32),
            pltpu.SMEM((16, CAP), I32),
            pltpu.SemaphoreType.DMA((9,)),
            pltpu.SemaphoreType.DMA((len(OFFSETS),)),
            pltpu.SemaphoreType.DMA((len(OFFSETS),)),
        ],
        compiler_params=params(4, 0),
        name="halo",
    )(send, coords, weight, lists, counts, centers, width, density, variance)


def unpack(word):
    return lax.shift_right_logical(word, 20), lax.shift_right_logical(word, 10) & 1023, word & 1023


def exponents(flat, rates, feats, at):
    t, b1, b2 = unpack(flat[0, at])
    pair = jnp.concatenate([feats[b1], feats[b2]], axis=1)
    ones = jnp.ones((16, 256), BF)
    return jnp.dot(
        rates[t], jnp.concatenate([pair, pair, ones], axis=0), preferred_element_type=F32
    )


def turns_of(count, turns):
    return lax.div(count + (turns - 1), turns)


def weighed(flat, weights, at, k):
    t, b1, b2 = unpack(flat[0, at])
    return t, k[:, :128] * weights[pl.ds(b1, 1), :] + k[:, 128:] * weights[pl.ds(b2, 1), :]


def rest_kernel(turns, depth, flat, rates, feats, weights, total, power):
    count = flat[0, FLAT - 1]
    for t in range(TILES):
        total[t] = jnp.zeros((128, 128), F32)
    for d in range(depth):
        power[d] = exponents(flat, rates, feats, FIXED + d)

    def body(i, carry):
        first = FIXED + turns * i
        for u in range(turns):
            power[(u + depth) % turns] = exponents(flat, rates, feats, first + u + depth)
            t, more = weighed(flat, weights, first + u, jnp.exp2(power[u]))
            total[t] += more
        return carry

    lax.fori_loop(0, turns_of(count, turns), body, 0)


def rest_pass(flat, rates, feats, weights):
    turns, depth = 16, 4
    return pl.pallas_call(
        functools.partial(rest_kernel, turns, depth),
        out_shape=jax.ShapeDtypeStruct((TILES, 128, 128), F32),
        in_specs=[SMEM, VMEM, VMEM, VMEM],
        out_specs=VMEM,
        scratch_shapes=[pltpu.VMEM((turns, 128, 256), F32)],
        compiler_params=params(4),
        name="rest_pass",
    )(flat, rates, feats, weights)


def raise_(value, split, src):
    k = jnp.exp2(value)
    hi = k.astype(BF)
    split[src, :128] = hi
    split[src, 128:] = (k - hi.astype(F32)).astype(BF)


def main_kernel(
    bunch, ahead, flat, rates, feats, weights, begun, centers, width, density, variance,
    mean_ref, pull_ref, both_ref, power, split, total, model, slots, lines, send_sem, recv_sem,
):
    rep, sp = lax.axis_index("rep"), lax.axis_index("sp")
    peers = [(lax.rem(rep + d, 8), sp) for d in range(1, 8)]
    barrier = pltpu.get_barrier_semaphore()
    for peer in peers:
        pl.semaphore_signal(barrier, inc=1, device_id=peer, device_id_type=MESH)
    per_group = TILES // GROUPS
    turns = bunch * SURE
    for d in range(ahead):
        power[d] = exponents(flat, rates, feats, d)

    def send(group):
        rows = pl.ds(pl.multiple_of(per_group * group, 8), per_group)
        return [
            pltpu.make_async_remote_copy(
                src_ref=model.at[rows],
                dst_ref=slots.at[rep, rows],
                send_sem=send_sem.at[group, d],
                recv_sem=recv_sem.at[group, d],
                device_id=peer,
                device_id_type=MESH,
            )
            for d, peer in enumerate(peers)
        ]

    def first_pass(group, carry):
        def body(i, carry):
            tile = per_group * group + bunch * i
            first = tile * SURE
            for u in range(turns):
                power[first + u + ahead] = exponents(flat, rates, feats, first + u + ahead)
                own_tile = u // SURE
                unused_t, more = weighed(flat, weights, first + u, jnp.exp2(power[first + u]))
                if u % SURE == 0:
                    total[own_tile] = begun[tile + own_tile] + more
                else:
                    total[own_tile] += more
            for j in range(bunch):
                model[pl.ds(tile + j, 1), :] = jnp.sum(total[j], axis=-1)[None, :]
            return carry

        lax.fori_loop(0, per_group // bunch, body, 0)

        @pl.when(group == 0)
        def _():
            pl.semaphore_wait(barrier, 7)

        for copy in send(group):
            copy.start()
        return carry

    lax.fori_loop(0, GROUPS, first_pass, 0)
    lines[...] = jnp.zeros((per_group * 16, 128), F32)
    for d in range(2):
        raise_(power[d], split, d)

    def second_pass(group, carry):
        rows = pl.ds(pl.multiple_of(per_group * group, 8), per_group)
        slots[rep, rows] = model[rows, :]
        for copy in send(group):
            copy.wait()
        sum_ = slots[0, rows]
        for r in range(1, 8):
            sum_ = sum_ + slots[r, rows]
        mean = sum_ * 0.125
        mean_ref[rows, :] = mean
        rate = (mean - density[rows, :]) / variance[rows, :] * width[rows, :]
        for row, value in enumerate([rate] + [rate * centers[c, rows] for c in range(3)]):
            hi = value.astype(BF).astype(F32)
            lines[pl.ds(row, 8, stride=16), :] = hi
            lines[pl.ds(4 + row, 8, stride=16), :] = value - hi
        for j in range(per_group):
            eight = lines[16 * j : 16 * j + 16, :].astype(BF)
            pull_ref[per_group * group + j] = jnp.concatenate([eight, eight], axis=1)

        def body(i, carry):
            tile = per_group * group + bunch * i
            first = tile * SURE
            for u in range(turns):
                raise_(power[first + u + 2], split, (u + 2) % RING)
                both_ref[first + u] = jnp.dot(
                    pull_ref[tile + u // SURE], split[u % RING], preferred_element_type=F32
                )[:8]
            return carry

        lax.fori_loop(0, per_group // bunch, body, 0)
        return carry

    lax.fori_loop(0, GROUPS, second_pass, 0)


def main_pass(flat, rates, feats, weights, begun, centers, width, density, variance):
    bunch, ahead = 4, 4
    return pl.pallas_call(
        functools.partial(main_kernel, bunch, ahead),
        out_shape=(
            jax.ShapeDtypeStruct((TILES, 128), F32),
            jax.ShapeDtypeStruct((TILES, 16, 256), BF),
            jax.ShapeDtypeStruct((FIXED, 8, 256), F32),
        ),
        in_specs=[SMEM] + [VMEM] * 8,
        out_specs=(VMEM, VMEM, VMEM),
        scratch_shapes=[
            pltpu.VMEM((FIXED + ahead, 128, 256), F32),
            pltpu.VMEM((RING, 256, 256), BF),
            pltpu.VMEM((bunch, 128, 128), F32),
            pltpu.VMEM((TILES, 128), F32),
            pltpu.VMEM((8, TILES, 128), F32),
            pltpu.VMEM((TILES // GROUPS * 16, 128), F32),
            pltpu.SemaphoreType.DMA((GROUPS, 7)),
            pltpu.SemaphoreType.DMA((GROUPS, 7)),
        ],
        compiler_params=params(44, 1),
        name="main_pass",
    )(flat, rates, feats, weights, begun, centers, width, density, variance)


def summed(moments, first):
    return [
        moments[pl.ds(8 * first + c, 8, stride=8), :]
        + moments[pl.ds(8 * first + 4 + c, 8, stride=8), :]
        for c in range(4)
    ]


def force_kernel(turns, flat, rates, feats, pulls, both_ref, received, slot_ref, moments, power, split):
    count = flat[0, FLAT - 1]

    def clear(i, carry):
        moments[pl.ds(pl.multiple_of(128 * i, 128), 128), :] = jnp.zeros((128, 128), F32)
        return carry

    lax.fori_loop(0, ROWS // 16, clear, 0)

    def put(at, both):
        unused_t, b1, b2 = unpack(flat[0, at])
        moments[pl.ds(pl.multiple_of(8 * b1, 8), 8), :] += both[:8, :128]
        moments[pl.ds(pl.multiple_of(8 * b2, 8), 8), :] += both[:8, 128:]

    def known(i, carry):
        for u in range(8):
            put(8 * i + u, both_ref[8 * i + u])
        return carry

    lax.fori_loop(0, FIXED // 8, known, 0)
    for d in range(4):
        power[d] = exponents(flat, rates, feats, FIXED + d)
    for d in range(2):
        raise_(power[d], split, d)

    def body(i, carry):
        first = FIXED + turns * i
        for u in range(turns):
            power[(u + 4) % turns] = exponents(flat, rates, feats, first + u + 4)
            raise_(power[(u + 2) % turns], split, (u + 2) % turns)
            t = lax.shift_right_logical(flat[0, first + u], 20)
            put(first + u, jnp.dot(pulls[t], split[u % turns], preferred_element_type=F32))
        return carry

    lax.fori_loop(0, turns_of(count, turns), body, 0)
    for p in range(len(OFFSETS)):
        for h in range(CAP // 8):
            four = summed(moments, OWN + p * CAP + 8 * h)
            at = p * 4 * CAP + 8 * h
            twice = 2.0 * received[at + 3 * CAP : at + 3 * CAP + 8, :]
            for c in range(3):
                xyz = received[at + c * CAP : at + c * CAP + 8, :]
                to = p * BACK + c * CAP + 8 * h
                slot_ref[to : to + 8, :] = twice * (xyz * four[0] - four[1 + c])


def force_pass(flat, rates, feats, pulls, both, received):
    turns = 16
    return pl.pallas_call(
        functools.partial(force_kernel, turns),
        out_shape=(
            jax.ShapeDtypeStruct((3 * HALO, 128), F32),
            jax.ShapeDtypeStruct((ROWS * 8, 128), F32),
        ),
        in_specs=[SMEM] + [VMEM] * 5,
        out_specs=(VMEM, VMEM),
        scratch_shapes=[
            pltpu.VMEM((turns, 128, 256), F32),
            pltpu.VMEM((turns, 256, 256), BF),
        ],
        compiler_params=params(6),
        name="force_pass",
    )(flat, rates, feats, pulls, both, received)


def return_kernel(slot_ref, moments, coords, weights, out_ref, own_ref, send_sem, recv_sem):
    greet([sp_peer(o) for o in OFFSETS])
    copies = []
    for p, offset in enumerate(OFFSETS):
        copy = pltpu.make_async_remote_copy(
            src_ref=slot_ref.at[pl.ds(p * BACK, BACK)],
            dst_ref=out_ref.at[pl.ds(p * BACK, BACK)],
            send_sem=send_sem.at[p],
            recv_sem=recv_sem.at[p],
            device_id=sp_peer(offset),
            device_id_type=MESH,
        )
        copy.start()
        copies.append(copy)

    def own(i, carry):
        for u in range(4):
            b = pl.multiple_of(32 * i + 8 * u, 8)
            four = summed(moments, b)
            twice = 2.0 * weights[pl.ds(b, 8), :]
            for c in range(3):
                own_ref[c, pl.ds(b, 8), :] = twice * (coords[c, pl.ds(b, 8), :] * four[0] - four[1 + c])
        return carry

    lax.fori_loop(0, OWN // 32, own, 0)
    for copy in copies:
        copy.wait()


def return_forces(slots, moments, coords, weights):
    return pl.pallas_call(
        return_kernel,
        out_shape=(
            jax.ShapeDtypeStruct((3 * HALO, 128), F32),
            jax.ShapeDtypeStruct((3, OWN, 128), F32),
        ),
        in_specs=[VMEM] * 4,
        out_specs=(VMEM, VMEM),
        scratch_shapes=[
            pltpu.SemaphoreType.DMA((len(OFFSETS),)),
            pltpu.SemaphoreType.DMA((len(OFFSETS),)),
        ],
        compiler_params=params(4, 2),
        name="return_forces",
    )(slots, moments, coords, weights)


def merge_kernel(send_ref, own_ref, back_ref, out_ref):
    out_ref[...] = own_ref[...]
    me = lax.axis_index("sp")
    for p, offset in enumerate(OFFSETS):
        to = lax.rem(me + 16 - offset, 16)
        for k in range(CAP):
            b = send_ref[to, k]
            for c in range(3):
                row = p * BACK + c * CAP + k
                out_ref[c, pl.ds(b, 1), :] += back_ref[row : row + 1, :]


def merge(send, own, back):
    return pl.pallas_call(
        merge_kernel,
        out_shape=jax.ShapeDtypeStruct((3, OWN, 128), F32),
        in_specs=[SMEM, VMEM, VMEM],
        out_specs=VMEM,
        compiler_params=params(4),
        name="merge",
    )(send, own, back)


def local(
    coords, atom_weight, centers, inv_width, density, variance, tile_blocks, tile_counts, send_blocks
):
    own, send = jnp.transpose(coords[0], (1, 0, 2)), send_blocks[0]
    centers = jnp.transpose(centers, (1, 0, 2))
    given = (send, own, atom_weight, tile_blocks, tile_counts[None], centers, inv_width, density, variance)
    received, feats, rates, weights, flat, own, centers, width, density, variance = halo(
        *[pltpu.with_memory_space_constraint(x, pltpu.HBM) for x in given]
    )
    begun = rest_pass(flat, rates, feats, weights)
    mean, pulls, both = main_pass(
        flat, rates, feats, weights, begun, centers, width, density, variance
    )
    slots, moments = force_pass(flat, rates, feats, pulls, both, received)
    back, forces = return_forces(slots, moments, own, weights)
    return jnp.transpose(merge(send, forces, back), (1, 0, 2))[None], mean


def solution(mesh):
    return jax.shard_map(
        local,
        mesh=mesh,
        in_specs=(
            P("rep", "sp", None, None),
            P("sp", None),
            P("sp", None, None),
            P("sp", None),
            P("sp", None),
            P("sp", None),
            P("sp", None),
            P("sp"),
            P("sp", None, None),
        ),
        out_specs=(P("rep", "sp", None, None), P("sp", None)),
        check_vma=False,
    )
```

```python
import functools

import jax
import jax.numpy as jnp
from jax import lax
from jax.experimental import pallas as pl
from jax.experimental.pallas import tpu as pltpu
from jax.sharding import PartitionSpec as P

MESH = pl.DeviceIdType.MESH
BF = jnp.bfloat16
F32 = jnp.float32
I32 = jnp.int32
VMEM = pl.BlockSpec(memory_space=pltpu.VMEM)
SMEM = pl.BlockSpec(memory_space=pltpu.SMEM)
HBM = pl.BlockSpec(memory_space=pltpu.HBM)

OFFSETS = (1, 2, 3, 8, 13, 14, 15)
CAP = 16
OWN = 512
HALO = len(OFFSETS) * CAP
TABLE = OWN + HALO
DUMMY = TABLE
ROWS = TABLE + CAP
TILES = 32
LIST = 32
STEPS = TILES * LIST // 2
GROUPS = 4
TILES_OF = TILES // GROUPS
STEPS_OF = STEPS // GROUPS
PAIRS_OF = TILES_OF * LIST
BUNCH = 4
BACK = 3 * CAP
DEPTH = 48
LOG2E = 1.4426950408889634


def params(limit_mib, collective_id=None):
    more = {} if collective_id is None else {"collective_id": collective_id, "has_side_effects": True}
    return pltpu.CompilerParams(vmem_limit_bytes=limit_mib << 20, **more)


def sp_peer(offset):
    return (lax.axis_index("rep"), lax.rem(lax.axis_index("sp") + offset, 16))


def pieces(x):
    hi = x.astype(BF).astype(F32)
    rest = x - hi
    mid = rest.astype(BF).astype(F32)
    return hi, mid, rest - mid


def put_features(xyz, feats, first, lines, at):
    square = xyz[0] * xyz[0] + xyz[1] * xyz[1] + xyz[2] * xyz[2]
    for row, value in enumerate((*xyz, square)):
        hi, mid, lo = pieces(value)
        for group, piece in enumerate((hi, mid, hi, lo)):
            lines[pl.ds(at * 128 + 4 * group + row, 8, stride=16), :] = piece
    for b in range(8):
        feats[first + b] = lines[at * 128 + 16 * b : at * 128 + 16 * b + 16, :].astype(BF)


def put_rates(centers, width, rates, lines):
    slope = width[...] * LOG2E
    x = [centers[c] for c in range(3)]
    size = x[0] * x[0] + x[1] * x[1] + x[2] * x[2]
    zero = jnp.zeros((TILES, 128), F32)
    rows = [zero] * DEPTH
    for c, value in enumerate([2.0 * slope * x[0], 2.0 * slope * x[1], 2.0 * slope * x[2], -slope]):
        hi, mid, lo = pieces(value)
        for group, piece in enumerate((hi, hi, mid, hi, lo, mid)):
            rows[4 * group + c] = piece
    for at, piece in enumerate(pieces(-slope * size)):
        rows[32 + at] = piece
    for r in range(DEPTH):
        for q in range(TILES // 8):
            lines[pl.ds(8 * q * DEPTH + r, 8, stride=DEPTH), :] = rows[r][8 * q : 8 * q + 8]

    def tile(t, carry):
        block = lines[pl.ds(pl.multiple_of(t * DEPTH, 8), DEPTH), :]
        rates[t] = jnp.transpose(block).astype(BF)
        return carry

    lax.fori_loop(0, TILES, tile, 0, unroll=4)


def table_ids(lists, counts, ids):
    me = lax.axis_index("sp")
    named = lists[...]
    slot = named - OWN
    offset = (lax.shift_right_arithmetic(slot, 4) - me) & 15
    place = jnp.where(offset < 4, offset - 1, jnp.where(offset == 8, 3, offset - 9))
    named = jnp.where(slot < 0, named, OWN + place * CAP + (slot & (CAP - 1)))
    row = jnp.broadcast_to(counts[...], (TILES, TILES)).astype(F32)
    sub = lax.broadcasted_iota(I32, (TILES, TILES), 0)
    lane = lax.broadcasted_iota(I32, (TILES, TILES), 1)
    count = jnp.sum(jnp.where(lane == sub, row, 0.0), axis=1, keepdims=True)
    ids[...] = jnp.where(lane.astype(F32) < count, named, DUMMY)


def two_pieces(x):
    hi = x.astype(BF)
    return hi, (x - hi.astype(F32)).astype(BF)


def one_hot(rows, first, names):
    at = lax.broadcasted_iota(I32, (rows, names.shape[1]), 0) + first
    return jnp.where(at == names, 1.0, 0.0).astype(BF)


def restraint_kernel(
    send_hbm, coords_hbm, weight_hbm, lists_hbm, counts_hbm, centers_hbm, width_hbm, density_hbm, variance_hbm,
    force_ref, mean_ref,
    coords, weights, centers, width, density, variance, lists, counts, send_rows, send_ref,
    ids, names, ids_smem, pack, received, feats, rates, lines, power, total, model, slots, pulls,
    entries, moments, away, back,
    near_sem, halo_send, halo_recv, rep_send, rep_recv, back_send, back_recv,
):
    rep, me = lax.axis_index("rep"), lax.axis_index("sp")
    rep_peers = [(lax.rem(rep + d, 8), me) for d in range(1, 8)]
    barrier = pltpu.get_barrier_semaphore()
    for peer in [sp_peer(o) for o in OFFSETS] + rep_peers:
        pl.semaphore_signal(barrier, inc=1, device_id=peer, device_id_type=MESH)
    near = [
        pltpu.make_async_copy(src, dst, near_sem.at[i])
        for i, (src, dst) in enumerate((
            (send_hbm, send_ref),
            (coords_hbm, coords),
            (weight_hbm, weights.at[pl.ds(0, OWN)]),
            (lists_hbm, lists),
            (counts_hbm, counts),
            (centers_hbm, centers),
            (width_hbm, width),
            (density_hbm, density),
            (variance_hbm, variance),
            (send_hbm, send_rows),
        ))
    ]
    for copy in near:
        copy.start()
    for copy in near[:3]:
        copy.wait()

    halo_copies = []
    for p, offset in enumerate(OFFSETS):
        to = lax.rem(me + 16 - offset, 16)
        for k in range(CAP):
            b = send_ref[to, k]
            for c in range(3):
                row = (p * 4 + c) * CAP + k
                pack[row : row + 1, :] = coords[c, pl.ds(b, 1), :]
            row = (p * 4 + 3) * CAP + k
            pack[row : row + 1, :] = weights[pl.ds(b, 1), :]
        if p == 0:
            pl.semaphore_wait(barrier, len(OFFSETS) + 7)
        copy = pltpu.make_async_remote_copy(
            src_ref=pack.at[pl.ds(p * 4 * CAP, 4 * CAP)],
            dst_ref=received.at[pl.ds(p * 4 * CAP, 4 * CAP)],
            send_sem=halo_send.at[p],
            recv_sem=halo_recv.at[p],
            device_id=sp_peer(16 - offset),
            device_id_type=MESH,
        )
        copy.start()
        halo_copies.append(copy)

    for copy in near[3:]:
        copy.wait()
    table_ids(lists, counts, ids)
    to_smem = pltpu.make_async_copy(ids, ids_smem, near_sem.at[10])
    to_smem.start()
    put_rates(centers, width, rates, lines)
    for g in range(GROUPS):
        for j in range(TILES_OF):
            names[g : g + 1, LIST * j : LIST * j + LIST] = ids[TILES_OF * g + j : TILES_OF * g + j + 1, :]
    weights[TABLE:ROWS, :] = jnp.zeros((ROWS - TABLE, 128), F32)
    for b in range(TABLE, ROWS):
        feats[b] = jnp.zeros((16, 128), BF)

    def own_features(i, carry):
        for u in range(4):
            b = pl.multiple_of(32 * i + 8 * u, 8)
            put_features([coords[c, pl.ds(b, 8), :] for c in range(3)], feats, b, lines, u)
        return carry

    lax.fori_loop(0, OWN // 32, own_features, 0)
    to_smem.wait()
    for p, copy in enumerate(halo_copies):
        copy.wait()
        for h in range(CAP // 8):
            rows = [
                received[(p * 4 + c) * CAP + 8 * h : (p * 4 + c) * CAP + 8 * h + 8, :]
                for c in range(4)
            ]
            first = OWN + p * CAP + 8 * h
            put_features(rows[:3], feats, first, lines, (2 * p + h) % 4)
            weights[first : first + 8, :] = rows[3]
    lines[0 : TILES_OF * 16, :] = jnp.zeros((TILES_OF * 16, 128), F32)
    ones = jnp.ones((16, 256), BF)

    def replicas(group):
        rows = pl.ds(pl.multiple_of(TILES_OF * group, 8), TILES_OF)
        return [
            pltpu.make_async_remote_copy(
                src_ref=model.at[rows],
                dst_ref=slots.at[rep, rows],
                send_sem=rep_send.at[group, d],
                recv_sem=rep_recv.at[group, d],
                device_id=peer,
                device_id_type=MESH,
            )
            for d, peer in enumerate(rep_peers)
        ]

    def first_pass(group):
        def body(i, carry):
            tile = TILES_OF * group + BUNCH * i
            place = STEPS_OF * lax.rem(group, 2) + BUNCH * (LIST // 2) * i
            for j in range(BUNCH):
                for s in range(LIST // 2):
                    b1, b2 = ids_smem[tile + j, 2 * s], ids_smem[tile + j, 2 * s + 1]
                    pair = jnp.concatenate([feats[b1], feats[b2]], axis=1)
                    k = jnp.exp2(
                        jnp.dot(
                            rates[tile + j],
                            jnp.concatenate([pair, pair, ones], axis=0),
                            preferred_element_type=F32,
                        )
                    )
                    power[place + j * (LIST // 2) + s] = k
                    more = (
                        k[:, :128] * weights[pl.ds(b1, 1), :] + k[:, 128:] * weights[pl.ds(b2, 1), :]
                    )
                    if s == 0:
                        total[j] = more
                    else:
                        total[j] += more
            for j in range(BUNCH):
                model[pl.ds(tile + j, 1), :] = jnp.sum(total[j], axis=-1)[None, :]
            return carry

        lax.fori_loop(0, TILES_OF // BUNCH, body, 0)
        for copy in replicas(group):
            copy.start()

    def second_pass(group):
        rows = pl.ds(pl.multiple_of(TILES_OF * group, 8), TILES_OF)
        slots[rep, rows] = model[rows, :]
        for copy in replicas(group):
            copy.wait()
        sum_ = slots[0, rows]
        for r in range(1, 8):
            sum_ = sum_ + slots[r, rows]
        mean = sum_ * 0.125
        mean_ref[rows, :] = mean
        rate = (mean - density[rows, :]) / variance[rows, :] * width[rows, :]
        for row, value in enumerate([rate] + [rate * centers[c, rows] for c in range(3)]):
            hi = value.astype(BF).astype(F32)
            lines[pl.ds(row, 8, stride=16), :] = hi
            lines[pl.ds(4 + row, 8, stride=16), :] = value - hi
        for j in range(TILES_OF):
            eight = lines[16 * j : 16 * j + 16, :].astype(BF)
            pulls[j] = jnp.concatenate([eight, eight], axis=1)

        def body(i, carry):
            place = STEPS_OF * lax.rem(group, 2) + BUNCH * (LIST // 2) * i
            entry = (TILES_OF * group + BUNCH * i) * LIST
            for j in range(BUNCH):
                for s in range(LIST // 2):
                    k = power[place + j * (LIST // 2) + s]
                    hi, lo = two_pieces(k)
                    both = jnp.dot(
                        pulls[BUNCH * i + j],
                        jnp.concatenate([hi, lo], axis=0),
                        preferred_element_type=F32,
                    )
                    at = entry + j * LIST + 2 * s
                    entries[at] = both[:8, :128]
                    entries[at + 1] = both[:8, 128:]
            return carry

        lax.fori_loop(0, TILES_OF // BUNCH, body, 0)

    def turn(i, carry):
        @pl.when(i < GROUPS)
        def _():
            first_pass(i)

        @pl.when(i > 0)
        def _():
            second_pass(i - 1)

        return carry

    lax.fori_loop(0, GROUPS + 1, turn, 0)

    def collect(rows, first):
        def body(g, carry):
            hot = one_hot(rows, first, names[pl.ds(g, 1), :])
            for half in range(2):
                parts = []
                for c in (2 * half, 2 * half + 1):
                    x = sum_rows(g, c)
                    parts.append(two_pieces(x))
                hi = jnp.concatenate([parts[0][0], parts[1][0]], axis=1)
                lo = jnp.concatenate([parts[0][1], parts[1][1]], axis=1)
                got = jnp.dot(hot, hi, preferred_element_type=F32) + jnp.dot(
                    hot, lo, preferred_element_type=F32
                )
                for q in range(2):
                    moments[2 * half + q, first : first + rows, :] += got[:, 128 * q : 128 * q + 128]
            return carry

        def sum_rows(g, c):
            flat = entries.reshape(TILES * LIST * 8, 128)
            at = pl.multiple_of(g * PAIRS_OF * 8, 8)
            return (
                flat[pl.ds(at + c, PAIRS_OF, stride=8), :]
                + flat[pl.ds(at + 4 + c, PAIRS_OF, stride=8), :]
            )

        for c in range(4):
            moments[c, first : first + rows, :] = jnp.zeros((rows, 128), F32)
        lax.fori_loop(0, GROUPS, body, 0)

    collect(HALO, OWN)
    for p in range(len(OFFSETS)):
        from_ = OWN + p * CAP
        at = p * 4 * CAP
        twice = 2.0 * received[at + 3 * CAP : at + 4 * CAP, :]
        for c in range(3):
            xyz = received[at + c * CAP : at + c * CAP + CAP, :]
            to = p * BACK + c * CAP
            away[to : to + CAP, :] = twice * (
                xyz * moments[0, from_ : from_ + CAP, :] - moments[1 + c, from_ : from_ + CAP, :]
            )
    back_copies = []
    for p, offset in enumerate(OFFSETS):
        copy = pltpu.make_async_remote_copy(
            src_ref=away.at[pl.ds(p * BACK, BACK)],
            dst_ref=back.at[pl.ds(p * BACK, BACK)],
            send_sem=back_send.at[p],
            recv_sem=back_recv.at[p],
            device_id=sp_peer(offset),
            device_id_type=MESH,
        )
        copy.start()
        back_copies.append(copy)
    collect(OWN, 0)
    for copy in back_copies:
        copy.wait()
    sent = [send_rows[pl.ds(lax.rem(me + 16 - offset, 16), 1), :] for offset in OFFSETS]
    hot = one_hot(OWN, 0, jnp.concatenate(sent + [jnp.full((1, 128 - HALO), -1, I32)], axis=1))
    twice = 2.0 * weights[0:OWN, :]
    for c in range(3):
        rows = [back[p * BACK + c * CAP : p * BACK + c * CAP + CAP, :] for p in range(len(OFFSETS))]
        hi, lo = two_pieces(jnp.concatenate(rows + [jnp.zeros((128 - HALO, 128), F32)], axis=0))
        got = jnp.dot(
            jnp.concatenate([hot, hot], axis=1),
            jnp.concatenate([hi, lo], axis=0),
            preferred_element_type=F32,
        )
        force_ref[c] = got + twice * (coords[c] * moments[0, 0:OWN, :] - moments[1 + c, 0:OWN, :])


def restraint(*given):
    dma = pltpu.SemaphoreType.DMA
    peers = len(OFFSETS)
    tiles = pltpu.VMEM((TILES, 128), F32)
    return pl.pallas_call(
        restraint_kernel,
        out_shape=(
            jax.ShapeDtypeStruct((3, OWN, 128), F32),
            jax.ShapeDtypeStruct((TILES, 128), F32),
        ),
        in_specs=[HBM] * 9,
        out_specs=(VMEM,) * 2,
        scratch_shapes=[
            pltpu.VMEM((3, OWN, 128), F32),
            pltpu.VMEM((ROWS, 128), F32),
            pltpu.VMEM((3, TILES, 128), F32),
            tiles,
            tiles,
            tiles,
            pltpu.VMEM((TILES, LIST), I32),
            pltpu.VMEM((1, TILES), I32),
            pltpu.VMEM((16, CAP), I32),
            pltpu.SMEM((16, CAP), I32),
            pltpu.VMEM((TILES, LIST), I32),
            pltpu.VMEM((GROUPS, PAIRS_OF), I32),
            pltpu.SMEM((TILES, LIST), I32),
            pltpu.VMEM((4 * HALO, 128), F32),
            pltpu.VMEM((4 * HALO, 128), F32),
            pltpu.VMEM((ROWS, 16, 128), BF),
            pltpu.VMEM((TILES, 128, DEPTH), BF),
            pltpu.VMEM((TILES * DEPTH, 128), F32),
            pltpu.VMEM((2 * STEPS_OF, 128, 256), F32),
            pltpu.VMEM((BUNCH, 128, 128), F32),
            tiles,
            pltpu.VMEM((8, TILES, 128), F32),
            pltpu.VMEM((TILES_OF, 16, 256), BF),
            pltpu.VMEM((TILES * LIST, 8, 128), F32),
            pltpu.VMEM((4, TABLE, 128), F32),
            pltpu.VMEM((3 * HALO, 128), F32),
            pltpu.VMEM((3 * HALO, 128), F32),
            dma((11,)),
            dma((peers,)),
            dma((peers,)),
            dma((GROUPS, 7)),
            dma((GROUPS, 7)),
            dma((peers,)),
            dma((peers,)),
        ],
        compiler_params=params(58, 0),
        name="restraint",
    )(*given)


def local(
    coords, atom_weight, centers, inv_width, density, variance, tile_blocks, tile_counts, send_blocks
):
    own, send = jnp.transpose(coords[0], (1, 0, 2)), send_blocks[0]
    centers = jnp.transpose(centers, (1, 0, 2))
    given = (send, own, atom_weight, tile_blocks, tile_counts[None], centers, inv_width, density, variance)
    forces, mean = restraint(*[pltpu.with_memory_space_constraint(x, pltpu.HBM) for x in given])
    return jnp.transpose(forces, (1, 0, 2))[None], mean


def solution(mesh):
    return jax.shard_map(
        local,
        mesh=mesh,
        in_specs=(
            P("rep", "sp", None, None),
            P("sp", None),
            P("sp", None, None),
            P("sp", None),
            P("sp", None),
            P("sp", None),
            P("sp", None),
            P("sp"),
            P("sp", None, None),
        ),
        out_specs=(P("rep", "sp", None, None), P("sp", None)),
        check_vma=False,
    )
```

```python
import functools

import jax
import jax.numpy as jnp
from jax import lax
from jax.experimental import pallas as pl
from jax.experimental.pallas import tpu as pltpu
from jax.sharding import PartitionSpec as P

MESH = pl.DeviceIdType.MESH
BF = jnp.bfloat16
F32 = jnp.float32
I32 = jnp.int32
VMEM = pl.BlockSpec(memory_space=pltpu.VMEM)
SMEM = pl.BlockSpec(memory_space=pltpu.SMEM)
HBM = pl.BlockSpec(memory_space=pltpu.HBM)

OFFSETS = (1, 2, 3, 8, 13, 14, 15)
CAP = 16
OWN = 512
HALO = len(OFFSETS) * CAP
TABLE = OWN + HALO
DUMMY = TABLE
ROWS = TABLE + CAP
TILES = 32
LIST = 32
STEPS = TILES * LIST // 2
GROUPS = 8
LAG = 4
TILES_OF = TILES // GROUPS
STEPS_OF = STEPS // GROUPS
PAIRS_OF = 256
BATCHES = TILES * LIST // PAIRS_OF
BACK = 3 * CAP
DEPTH = 48
LOG2E = 1.4426950408889634


def params(limit_mib, collective_id=None):
    more = {} if collective_id is None else {"collective_id": collective_id, "has_side_effects": True}
    return pltpu.CompilerParams(vmem_limit_bytes=limit_mib << 20, **more)


def sp_peer(offset):
    return (lax.axis_index("rep"), lax.rem(lax.axis_index("sp") + offset, 16))


def pieces(x):
    hi = x.astype(BF).astype(F32)
    rest = x - hi
    mid = rest.astype(BF).astype(F32)
    return hi, mid, rest - mid


def put_features(xyz, feats, first, lines, at):
    square = xyz[0] * xyz[0] + xyz[1] * xyz[1] + xyz[2] * xyz[2]
    for row, value in enumerate((*xyz, square)):
        hi, mid, lo = pieces(value)
        for group, piece in enumerate((hi, mid, hi, lo)):
            lines[pl.ds(at * 128 + 4 * group + row, 8, stride=16), :] = piece
    for b in range(8):
        feats[first + b] = lines[at * 128 + 16 * b : at * 128 + 16 * b + 16, :].astype(BF)


def put_rates(centers, width, rates, lines):
    slope = width[...] * LOG2E
    x = [centers[c] for c in range(3)]
    size = x[0] * x[0] + x[1] * x[1] + x[2] * x[2]
    zero = jnp.zeros((TILES, 128), F32)
    rows = [zero] * DEPTH
    for c, value in enumerate([2.0 * slope * x[0], 2.0 * slope * x[1], 2.0 * slope * x[2], -slope]):
        hi, mid, lo = pieces(value)
        for group, piece in enumerate((hi, hi, mid, hi, lo, mid)):
            rows[4 * group + c] = piece
    for at, piece in enumerate(pieces(-slope * size)):
        rows[32 + at] = piece
    for r in range(DEPTH):
        for q in range(TILES // 8):
            lines[pl.ds(8 * q * DEPTH + r, 8, stride=DEPTH), :] = rows[r][8 * q : 8 * q + 8]

    def tile(t, carry):
        block = lines[pl.ds(pl.multiple_of(t * DEPTH, 8), DEPTH), :]
        rates[t] = jnp.transpose(block).astype(BF)
        return carry

    lax.fori_loop(0, TILES, tile, 0, unroll=4)


def table_ids(lists, counts, ids):
    me = lax.axis_index("sp")
    named = lists[...]
    slot = named - OWN
    offset = (lax.shift_right_arithmetic(slot, 4) - me) & 15
    place = jnp.where(offset < 4, offset - 1, jnp.where(offset == 8, 3, offset - 9))
    named = jnp.where(slot < 0, named, OWN + place * CAP + (slot & (CAP - 1)))
    row = jnp.broadcast_to(counts[...], (TILES, TILES)).astype(F32)
    sub = lax.broadcasted_iota(I32, (TILES, TILES), 0)
    lane = lax.broadcasted_iota(I32, (TILES, TILES), 1)
    count = jnp.sum(jnp.where(lane == sub, row, 0.0), axis=1, keepdims=True)
    ids[...] = jnp.where(lane.astype(F32) < count, named, DUMMY)


def two_pieces(x):
    hi = x.astype(BF)
    return hi, (x - hi.astype(F32)).astype(BF)


def one_hot(rows, first, names):
    at = lax.broadcasted_iota(I32, (rows, names.shape[1]), 0) + first
    return jnp.where(at == names, 1.0, 0.0).astype(BF)


def restraint_kernel(
    send_hbm, coords_hbm, weight_hbm, lists_hbm, counts_hbm, centers_hbm, width_hbm, density_hbm, variance_hbm,
    force_ref, mean_ref,
    coords, weights, centers, width, density, variance, lists, counts, send_rows, send_ref,
    ids, names, ids_smem, pack, received, feats, rates, lines, power, total, model, slots, means,
    entries, moments, away, back,
    near_sem, halo_send, halo_recv, rep_send, rep_recv, back_send, back_recv,
):
    rep, me = lax.axis_index("rep"), lax.axis_index("sp")
    rep_peers = [(lax.rem(rep + d, 8), me) for d in range(1, 8)]
    barrier = pltpu.get_barrier_semaphore()
    for peer in [sp_peer(o) for o in OFFSETS] + rep_peers:
        pl.semaphore_signal(barrier, inc=1, device_id=peer, device_id_type=MESH)
    near = [
        pltpu.make_async_copy(src, dst, near_sem.at[i])
        for i, (src, dst) in enumerate((
            (send_hbm, send_ref),
            (coords_hbm, coords),
            (weight_hbm, weights.at[pl.ds(0, OWN)]),
            (lists_hbm, lists),
            (counts_hbm, counts),
            (centers_hbm, centers),
            (width_hbm, width),
            (density_hbm, density),
            (variance_hbm, variance),
            (send_hbm, send_rows),
        ))
    ]
    for copy in near:
        copy.start()
    for copy in near[:3]:
        copy.wait()

    halo_copies = []
    for p, offset in enumerate(OFFSETS):
        to = lax.rem(me + 16 - offset, 16)
        for k in range(CAP):
            b = send_ref[to, k]
            for c in range(3):
                row = (p * 4 + c) * CAP + k
                pack[row : row + 1, :] = coords[c, pl.ds(b, 1), :]
            row = (p * 4 + 3) * CAP + k
            pack[row : row + 1, :] = weights[pl.ds(b, 1), :]
        if p == 0:
            pl.semaphore_wait(barrier, len(OFFSETS) + 7)
        copy = pltpu.make_async_remote_copy(
            src_ref=pack.at[pl.ds(p * 4 * CAP, 4 * CAP)],
            dst_ref=received.at[pl.ds(p * 4 * CAP, 4 * CAP)],
            send_sem=halo_send.at[p],
            recv_sem=halo_recv.at[p],
            device_id=sp_peer(16 - offset),
            device_id_type=MESH,
        )
        copy.start()
        halo_copies.append(copy)

    for copy in near[3:]:
        copy.wait()
    table_ids(lists, counts, ids)
    to_smem = pltpu.make_async_copy(ids, ids_smem, near_sem.at[10])
    to_smem.start()
    put_rates(centers, width, rates, lines)
    for t in range(TILES):
        g, j = divmod(t, PAIRS_OF // LIST)
        names[g : g + 1, LIST * j : LIST * j + LIST] = ids[t : t + 1, :]
    weights[TABLE:ROWS, :] = jnp.zeros((ROWS - TABLE, 128), F32)
    for b in range(TABLE, ROWS):
        feats[b] = jnp.zeros((16, 128), BF)

    def own_features(i, carry):
        for u in range(4):
            b = pl.multiple_of(32 * i + 8 * u, 8)
            put_features([coords[c, pl.ds(b, 8), :] for c in range(3)], feats, b, lines, u)
        return carry

    lax.fori_loop(0, OWN // 32, own_features, 0)
    to_smem.wait()
    for p, copy in enumerate(halo_copies):
        copy.wait()
        for h in range(CAP // 8):
            rows = [
                received[(p * 4 + c) * CAP + 8 * h : (p * 4 + c) * CAP + 8 * h + 8, :]
                for c in range(4)
            ]
            first = OWN + p * CAP + 8 * h
            put_features(rows[:3], feats, first, lines, (2 * p + h) % 4)
            weights[first : first + 8, :] = rows[3]
    lines[0 : TILES_OF * 16, :] = jnp.zeros((TILES_OF * 16, 128), F32)
    ones = jnp.ones((16, 256), BF)

    def replicas(group):
        return [
            pltpu.make_async_remote_copy(
                src_ref=model.at[group],
                dst_ref=slots.at[rep, group],
                send_sem=rep_send.at[group, d],
                recv_sem=rep_recv.at[group, d],
                device_id=peer,
                device_id_type=MESH,
            )
            for d, peer in enumerate(rep_peers)
        ]

    def first_pass(group):
        tile = TILES_OF * group
        place = STEPS_OF * lax.rem(group, LAG + 1)
        for j in range(TILES_OF):
            for s in range(LIST // 2):
                b1, b2 = ids_smem[tile + j, 2 * s], ids_smem[tile + j, 2 * s + 1]
                pair = jnp.concatenate([feats[b1], feats[b2]], axis=1)
                k = jnp.exp2(
                    jnp.dot(
                        rates[tile + j],
                        jnp.concatenate([pair, pair, ones], axis=0),
                        preferred_element_type=F32,
                    )
                )
                power[place + j * (LIST // 2) + s] = k
                more = (
                    k[:, :128] * weights[pl.ds(b1, 1), :] + k[:, 128:] * weights[pl.ds(b2, 1), :]
                )
                if s == 0:
                    total[j] = more
                else:
                    total[j] += more
        for j in range(TILES_OF):
            model[group, j : j + 1, :] = jnp.sum(total[j], axis=-1)[None, :]
        for copy in replicas(group):
            copy.start()

    def second_pass(group):
        rows = pl.ds(pl.multiple_of(TILES_OF * group, TILES_OF), TILES_OF)
        slots[rep, group] = model[group]
        for copy in replicas(group):
            copy.wait()
        sum_ = slots[0, group]
        for r in range(1, 8):
            sum_ = sum_ + slots[r, group]
        mean = sum_ * 0.125
        means[group] = mean
        rate = (mean - density[rows, :]) / variance[rows, :] * width[rows, :]
        for row, value in enumerate([rate] + [rate * centers[c, rows] for c in range(3)]):
            hi = value.astype(BF).astype(F32)
            lines[pl.ds(row, TILES_OF, stride=16), :] = hi
            lines[pl.ds(4 + row, TILES_OF, stride=16), :] = value - hi
        place = STEPS_OF * lax.rem(group, LAG + 1)
        entry = TILES_OF * group * LIST
        for j in range(TILES_OF):
            eight = lines[16 * j : 16 * j + 16, :].astype(BF)
            pull = jnp.concatenate([eight, eight], axis=1)
            for s in range(LIST // 2):
                hi, lo = two_pieces(power[place + j * (LIST // 2) + s])
                both = jnp.dot(pull, jnp.concatenate([hi, lo], axis=0), preferred_element_type=F32)
                four = both[:4] + both[4:8]
                at = entry + j * LIST + 2 * s
                entries[at] = four[:, :128]
                entries[at + 1] = four[:, 128:]

    def turn(i, carry):
        @pl.when(i < GROUPS)
        def _():
            first_pass(i)

        @pl.when(i >= LAG)
        def _():
            second_pass(i - LAG)

        return carry

    lax.fori_loop(0, GROUPS + LAG, turn, 0)
    for g in range(GROUPS):
        mean_ref[TILES_OF * g : TILES_OF * g + TILES_OF, :] = means[g]

    def collect(rows, first):
        def body(g, carry):
            hot = one_hot(rows, first, names[pl.ds(g, 1), :])
            for half in range(2):
                parts = []
                for c in (2 * half, 2 * half + 1):
                    x = sum_rows(g, c)
                    parts.append(two_pieces(x))
                hi = jnp.concatenate([parts[0][0], parts[1][0]], axis=1)
                lo = jnp.concatenate([parts[0][1], parts[1][1]], axis=1)
                got = jnp.dot(hot, hi, preferred_element_type=F32) + jnp.dot(
                    hot, lo, preferred_element_type=F32
                )
                for q in range(2):
                    moments[2 * half + q, first : first + rows, :] += got[:, 128 * q : 128 * q + 128]
            return carry

        def sum_rows(g, c):
            flat = entries.reshape(TILES * LIST * 4, 128)
            return flat[pl.ds(pl.multiple_of(g * PAIRS_OF * 4, 8) + c, PAIRS_OF, stride=4), :]

        for c in range(4):
            moments[c, first : first + rows, :] = jnp.zeros((rows, 128), F32)
        lax.fori_loop(0, BATCHES, body, 0)

    collect(HALO, OWN)
    for p in range(len(OFFSETS)):
        from_ = OWN + p * CAP
        at = p * 4 * CAP
        twice = 2.0 * received[at + 3 * CAP : at + 4 * CAP, :]
        for c in range(3):
            xyz = received[at + c * CAP : at + c * CAP + CAP, :]
            to = p * BACK + c * CAP
            away[to : to + CAP, :] = twice * (
                xyz * moments[0, from_ : from_ + CAP, :] - moments[1 + c, from_ : from_ + CAP, :]
            )
    back_copies = []
    for p, offset in enumerate(OFFSETS):
        copy = pltpu.make_async_remote_copy(
            src_ref=away.at[pl.ds(p * BACK, BACK)],
            dst_ref=back.at[pl.ds(p * BACK, BACK)],
            send_sem=back_send.at[p],
            recv_sem=back_recv.at[p],
            device_id=sp_peer(offset),
            device_id_type=MESH,
        )
        copy.start()
        back_copies.append(copy)
    collect(OWN, 0)
    for copy in back_copies:
        copy.wait()
    sent = [send_rows[pl.ds(lax.rem(me + 16 - offset, 16), 1), :] for offset in OFFSETS]
    hot = one_hot(OWN, 0, jnp.concatenate(sent + [jnp.full((1, 128 - HALO), -1, I32)], axis=1))
    twice = 2.0 * weights[0:OWN, :]
    for c in range(3):
        rows = [back[p * BACK + c * CAP : p * BACK + c * CAP + CAP, :] for p in range(len(OFFSETS))]
        hi, lo = two_pieces(jnp.concatenate(rows + [jnp.zeros((128 - HALO, 128), F32)], axis=0))
        got = jnp.dot(
            jnp.concatenate([hot, hot], axis=1),
            jnp.concatenate([hi, lo], axis=0),
            preferred_element_type=F32,
        )
        force_ref[c] = got + twice * (coords[c] * moments[0, 0:OWN, :] - moments[1 + c, 0:OWN, :])


def restraint(*given):
    dma = pltpu.SemaphoreType.DMA
    peers = len(OFFSETS)
    tiles = pltpu.VMEM((TILES, 128), F32)
    return pl.pallas_call(
        restraint_kernel,
        out_shape=(
            jax.ShapeDtypeStruct((3, OWN, 128), F32),
            jax.ShapeDtypeStruct((TILES, 128), F32),
        ),
        in_specs=[HBM] * 9,
        out_specs=(VMEM,) * 2,
        scratch_shapes=[
            pltpu.VMEM((3, OWN, 128), F32),
            pltpu.VMEM((ROWS, 128), F32),
            pltpu.VMEM((3, TILES, 128), F32),
            tiles,
            tiles,
            tiles,
            pltpu.VMEM((TILES, LIST), I32),
            pltpu.VMEM((1, TILES), I32),
            pltpu.VMEM((16, CAP), I32),
            pltpu.SMEM((16, CAP), I32),
            pltpu.VMEM((TILES, LIST), I32),
            pltpu.VMEM((BATCHES, PAIRS_OF), I32),
            pltpu.SMEM((TILES, LIST), I32),
            pltpu.VMEM((4 * HALO, 128), F32),
            pltpu.VMEM((4 * HALO, 128), F32),
            pltpu.VMEM((ROWS, 16, 128), BF),
            pltpu.VMEM((TILES, 128, DEPTH), BF),
            pltpu.VMEM((TILES * DEPTH, 128), F32),
            pltpu.VMEM(((LAG + 1) * STEPS_OF, 128, 256), F32),
            pltpu.VMEM((TILES_OF, 128, 128), F32),
            pltpu.VMEM((GROUPS, TILES_OF, 128), F32),
            pltpu.VMEM((8, GROUPS, TILES_OF, 128), F32),
            pltpu.VMEM((GROUPS, TILES_OF, 128), F32),
            pltpu.VMEM((TILES * LIST, 4, 128), F32),
            pltpu.VMEM((4, TABLE, 128), F32),
            pltpu.VMEM((3 * HALO, 128), F32),
            pltpu.VMEM((3 * HALO, 128), F32),
            dma((11,)),
            dma((peers,)),
            dma((peers,)),
            dma((GROUPS, 7)),
            dma((GROUPS, 7)),
            dma((peers,)),
            dma((peers,)),
        ],
        compiler_params=params(52, 0),
        name="restraint",
    )(*given)


def store_kernel(force_ref, mean_ref, force_hbm, mean_hbm, sems):
    copies = [pltpu.make_async_copy(mean_ref, mean_hbm, sems.at[0])]
    for c in range(3):
        for h in range(2):
            rows = pl.ds(OWN // 2 * h, OWN // 2)
            copies.append(
                pltpu.make_async_copy(
                    force_ref.at[c, rows], force_hbm.at[c, rows], sems.at[1 + 2 * c + h]
                )
            )
    for copy in copies:
        copy.start()
    for copy in copies:
        copy.wait()


def store(forces, mean):
    return pl.pallas_call(
        store_kernel,
        out_shape=(
            jax.ShapeDtypeStruct((3, OWN, 128), F32),
            jax.ShapeDtypeStruct((TILES, 128), F32),
        ),
        in_specs=[VMEM] * 2,
        out_specs=(HBM,) * 2,
        scratch_shapes=[pltpu.SemaphoreType.DMA((7,))],
        compiler_params=params(2),
        name="store",
    )(forces, mean)


def local(
    coords, atom_weight, centers, inv_width, density, variance, tile_blocks, tile_counts, send_blocks
):
    own, send = jnp.transpose(coords[0], (1, 0, 2)), send_blocks[0]
    centers = jnp.transpose(centers, (1, 0, 2))
    given = (send, own, atom_weight, tile_blocks, tile_counts[None], centers, inv_width, density, variance)
    forces, mean = store(
        *restraint(*[pltpu.with_memory_space_constraint(x, pltpu.HBM) for x in given])
    )
    return jnp.transpose(forces, (1, 0, 2))[None], mean


def solution(mesh):
    return jax.shard_map(
        local,
        mesh=mesh,
        in_specs=(
            P("rep", "sp", None, None),
            P("sp", None),
            P("sp", None, None),
            P("sp", None),
            P("sp", None),
            P("sp", None),
            P("sp", None),
            P("sp"),
            P("sp", None, None),
        ),
        out_specs=(P("rep", "sp", None, None), P("sp", None)),
        check_vma=False,
    )
```

```python
import functools

import jax
import jax.numpy as jnp
from jax import lax
from jax.experimental import pallas as pl
from jax.experimental.pallas import tpu as pltpu
from jax.sharding import PartitionSpec as P

MESH = pl.DeviceIdType.MESH
BF = jnp.bfloat16
F32 = jnp.float32
I32 = jnp.int32
VMEM = pl.BlockSpec(memory_space=pltpu.VMEM)
SMEM = pl.BlockSpec(memory_space=pltpu.SMEM)
HBM = pl.BlockSpec(memory_space=pltpu.HBM)

OFFSETS = (1, 2, 3, 8, 13, 14, 15)
CAP = 16
SENT_ORDER = (0, 1, 2, 3, 4, 5, 6)
WAIT_ORDER = (0, 6, 3, 2, 4, 1, 5)
BACK_ORDER = (1, 0, 2, 3, 5, 4, 6)
OWN = 512
HALO = len(OFFSETS) * CAP
TABLE = OWN + HALO
DUMMY = TABLE
ROWS = TABLE + CAP
TILES = 32
LIST = 32
STEPS = TILES * LIST // 2
GROUPS = 8
LAG = 4
TILES_OF = TILES // GROUPS
STEPS_OF = STEPS // GROUPS
PAIRS_OF = 256
BATCHES = TILES * LIST // PAIRS_OF
BACK = 3 * CAP
DEPTH = 48
LOG2E = 1.4426950408889634


def params(limit_mib, collective_id=None):
    more = {} if collective_id is None else {"collective_id": collective_id, "has_side_effects": True}
    return pltpu.CompilerParams(vmem_limit_bytes=limit_mib << 20, **more)


def sp_peer(offset):
    return (lax.axis_index("rep"), lax.rem(lax.axis_index("sp") + offset, 16))


def pieces(x):
    hi = x.astype(BF).astype(F32)
    rest = x - hi
    mid = rest.astype(BF).astype(F32)
    return hi, mid, rest - mid


def put_features(xyz, feats, first, lines, at):
    square = xyz[0] * xyz[0] + xyz[1] * xyz[1] + xyz[2] * xyz[2]
    for row, value in enumerate((*xyz, square)):
        hi, mid, lo = pieces(value)
        for group, piece in enumerate((hi, mid, hi, lo)):
            lines[pl.ds(at * 128 + 4 * group + row, 8, stride=16), :] = piece
    for b in range(8):
        feats[first + b] = lines[at * 128 + 16 * b : at * 128 + 16 * b + 16, :].astype(BF)


def put_rates(centers, width, rates, lines):
    slope = width[...] * LOG2E
    x = [centers[c] for c in range(3)]
    size = x[0] * x[0] + x[1] * x[1] + x[2] * x[2]
    zero = jnp.zeros((TILES, 128), F32)
    rows = [zero] * DEPTH
    for c, value in enumerate([2.0 * slope * x[0], 2.0 * slope * x[1], 2.0 * slope * x[2], -slope]):
        hi, mid, lo = pieces(value)
        for group, piece in enumerate((hi, hi, mid, hi, lo, mid)):
            rows[4 * group + c] = piece
    for at, piece in enumerate(pieces(-slope * size)):
        rows[32 + at] = piece
    for r in range(DEPTH):
        for q in range(TILES // 8):
            lines[pl.ds(8 * q * DEPTH + r, 8, stride=DEPTH), :] = rows[r][8 * q : 8 * q + 8]

    def tile(t, carry):
        block = lines[pl.ds(pl.multiple_of(t * DEPTH, 8), DEPTH), :]
        rates[t] = jnp.transpose(block).astype(BF)
        return carry

    lax.fori_loop(0, TILES, tile, 0, unroll=4)


def table_ids(lists, counts, ids):
    me = lax.axis_index("sp")
    named = lists[...]
    slot = named - OWN
    offset = (lax.shift_right_arithmetic(slot, 4) - me) & 15
    place = jnp.where(offset < 4, offset - 1, jnp.where(offset == 8, 3, offset - 9))
    named = jnp.where(slot < 0, named, OWN + place * CAP + (slot & (CAP - 1)))
    row = jnp.broadcast_to(counts[...], (TILES, TILES)).astype(F32)
    sub = lax.broadcasted_iota(I32, (TILES, TILES), 0)
    lane = lax.broadcasted_iota(I32, (TILES, TILES), 1)
    count = jnp.sum(jnp.where(lane == sub, row, 0.0), axis=1, keepdims=True)
    ids[...] = jnp.where(lane.astype(F32) < count, named, DUMMY)


def two_pieces(x):
    hi = x.astype(BF)
    return hi, (x - hi.astype(F32)).astype(BF)


def one_hot(rows, first, names):
    at = lax.broadcasted_iota(I32, (rows, names.shape[1]), 0) + first
    return jnp.where(at == names, 1.0, 0.0).astype(BF)


def restraint_kernel(
    send_hbm, coords_hbm, weight_hbm, lists_hbm, counts_hbm, centers_hbm, width_hbm, density_hbm, variance_hbm,
    force_ref, mean_ref,
    coords, weights, centers, width, density, variance, lists, counts, send_rows, send_ref,
    ids, names, ids_smem, pack, received, feats, rates, lines, power, total, model, slots, means,
    entries, moments, away, back, hots,
    near_sem, halo_send, halo_recv, rep_send, rep_recv, back_send, back_recv,
):
    rep, me = lax.axis_index("rep"), lax.axis_index("sp")
    rep_peers = [(lax.rem(rep + d, 8), me) for d in range(1, 8)]
    barrier = pltpu.get_barrier_semaphore()
    for peer in [sp_peer(o) for o in OFFSETS] + rep_peers:
        pl.semaphore_signal(barrier, inc=1, device_id=peer, device_id_type=MESH)
    near = [
        pltpu.make_async_copy(src, dst, near_sem.at[i])
        for i, (src, dst) in enumerate((
            (send_hbm, send_ref),
            (coords_hbm.at[0], coords.at[0]),
            (coords_hbm.at[1], coords.at[1]),
            (coords_hbm.at[2], coords.at[2]),
            (weight_hbm, weights.at[pl.ds(0, OWN)]),
            (lists_hbm, lists),
            (counts_hbm, counts),
            (centers_hbm, centers),
            (width_hbm, width),
            (density_hbm, density),
            (variance_hbm, variance),
            (send_hbm, send_rows),
        ))
    ]
    for copy in near:
        copy.start()
    for copy in near[:5]:
        copy.wait()

    halo_copies = {}
    for p in SENT_ORDER:
        offset = OFFSETS[p]
        to = lax.rem(me + 16 - offset, 16)
        for k in range(CAP):
            b = send_ref[to, k]
            for c in range(3):
                row = (p * 4 + c) * CAP + k
                pack[row : row + 1, :] = coords[c, pl.ds(b, 1), :]
            row = (p * 4 + 3) * CAP + k
            pack[row : row + 1, :] = weights[pl.ds(b, 1), :]
    pl.semaphore_wait(barrier, len(OFFSETS) + 7)
    for p in SENT_ORDER:
        offset = OFFSETS[p]
        copy = pltpu.make_async_remote_copy(
            src_ref=pack.at[pl.ds(p * 4 * CAP, 4 * CAP)],
            dst_ref=received.at[pl.ds(p * 4 * CAP, 4 * CAP)],
            send_sem=halo_send.at[p],
            recv_sem=halo_recv.at[p],
            device_id=sp_peer(16 - offset),
            device_id_type=MESH,
        )
        copy.start()
        halo_copies[p] = copy

    for copy in near[5:]:
        copy.wait()
    table_ids(lists, counts, ids)
    to_smem = pltpu.make_async_copy(ids, ids_smem, near_sem.at[12])
    to_smem.start()
    put_rates(centers, width, rates, lines)
    for t in range(TILES):
        g, j = divmod(t, PAIRS_OF // LIST)
        names[g : g + 1, LIST * j : LIST * j + LIST] = ids[t : t + 1, :]
    weights[TABLE:ROWS, :] = jnp.zeros((ROWS - TABLE, 128), F32)
    for b in range(TABLE, ROWS):
        feats[b] = jnp.zeros((16, 128), BF)

    def own_features(i, carry):
        for u in range(4):
            b = pl.multiple_of(32 * i + 8 * u, 8)
            put_features([coords[c, pl.ds(b, 8), :] for c in range(3)], feats, b, lines, u)
        return carry

    lax.fori_loop(0, OWN // 32, own_features, 0)
    to_smem.wait()
    for p in WAIT_ORDER:
        halo_copies[p].wait()
        for h in range(CAP // 8):
            rows = [
                received[(p * 4 + c) * CAP + 8 * h : (p * 4 + c) * CAP + 8 * h + 8, :]
                for c in range(4)
            ]
            first = OWN + p * CAP + 8 * h
            put_features(rows[:3], feats, first, lines, (2 * p + h) % 4)
            weights[first : first + 8, :] = rows[3]
    lines[0 : TILES_OF * 16, :] = jnp.zeros((TILES_OF * 16, 128), F32)
    ones = jnp.ones((16, 256), BF)

    def replicas(group):
        return [
            pltpu.make_async_remote_copy(
                src_ref=model.at[group],
                dst_ref=slots.at[rep, group],
                send_sem=rep_send.at[group, d],
                recv_sem=rep_recv.at[group, d],
                device_id=peer,
                device_id_type=MESH,
            )
            for d, peer in enumerate(rep_peers)
        ]

    def first_pass(group):
        tile = TILES_OF * group
        place = STEPS_OF * lax.rem(group, LAG + 1)
        for j in range(TILES_OF):
            for s in range(LIST // 2):
                b1, b2 = ids_smem[tile + j, 2 * s], ids_smem[tile + j, 2 * s + 1]
                pair = jnp.concatenate([feats[b1], feats[b2]], axis=1)
                k = jnp.exp2(
                    jnp.dot(
                        rates[tile + j],
                        jnp.concatenate([pair, pair, ones], axis=0),
                        preferred_element_type=F32,
                    )
                )
                power[place + j * (LIST // 2) + s] = k
                more = (
                    k[:, :128] * weights[pl.ds(b1, 1), :] + k[:, 128:] * weights[pl.ds(b2, 1), :]
                )
                if s == 0:
                    total[j] = more
                else:
                    total[j] += more
        for j in range(TILES_OF):
            model[group, j : j + 1, :] = jnp.sum(total[j], axis=-1)[None, :]
        for copy in replicas(group):
            copy.start()

    def second_pass(group):
        rows = pl.ds(pl.multiple_of(TILES_OF * group, TILES_OF), TILES_OF)
        slots[rep, group] = model[group]
        for copy in replicas(group):
            copy.wait()
        sum_ = slots[0, group]
        for r in range(1, 8):
            sum_ = sum_ + slots[r, group]
        mean = sum_ * 0.125
        means[group] = mean
        rate = (mean - density[rows, :]) / variance[rows, :] * width[rows, :]
        for row, value in enumerate([rate] + [rate * centers[c, rows] for c in range(3)]):
            hi = value.astype(BF).astype(F32)
            lines[pl.ds(row, TILES_OF, stride=16), :] = hi
            lines[pl.ds(4 + row, TILES_OF, stride=16), :] = value - hi
        place = STEPS_OF * lax.rem(group, LAG + 1)
        entry = TILES_OF * group * LIST
        for j in range(TILES_OF):
            eight = lines[16 * j : 16 * j + 16, :].astype(BF)
            pull = jnp.concatenate([eight, eight], axis=1)
            for s in range(LIST // 2):
                hi, lo = two_pieces(power[place + j * (LIST // 2) + s])
                both = jnp.dot(pull, jnp.concatenate([hi, lo], axis=0), preferred_element_type=F32)
                four = both[:4] + both[4:8]
                at = entry + j * LIST + 2 * s
                entries[at] = four[:, :128]
                entries[at + 1] = four[:, 128:]

    def turn(i, carry):
        @pl.when(i < GROUPS)
        def _():
            first_pass(i)

        @pl.when(i >= LAG)
        def _():
            second_pass(i - LAG)

        return carry

    lax.fori_loop(0, GROUPS + LAG, turn, 0)
    for g in range(GROUPS):
        mean_ref[TILES_OF * g : TILES_OF * g + TILES_OF, :] = means[g]

    def collect(rows, first):
        def body(g, carry):
            hot = one_hot(rows, first, names[pl.ds(g, 1), :])
            for half in range(2):
                parts = []
                for c in (2 * half, 2 * half + 1):
                    x = sum_rows(g, c)
                    parts.append(two_pieces(x))
                hi = jnp.concatenate([parts[0][0], parts[1][0]], axis=1)
                lo = jnp.concatenate([parts[0][1], parts[1][1]], axis=1)
                got = jnp.dot(hot, hi, preferred_element_type=F32) + jnp.dot(
                    hot, lo, preferred_element_type=F32
                )
                for q in range(2):
                    moments[2 * half + q, first : first + rows, :] += got[:, 128 * q : 128 * q + 128]
            return carry

        def sum_rows(g, c):
            flat = entries.reshape(TILES * LIST * 4, 128)
            return flat[pl.ds(pl.multiple_of(g * PAIRS_OF * 4, 8) + c, PAIRS_OF, stride=4), :]

        for c in range(4):
            moments[c, first : first + rows, :] = jnp.zeros((rows, 128), F32)
        lax.fori_loop(0, BATCHES, body, 0)

    collect(HALO, OWN)
    for p in range(len(OFFSETS)):
        from_ = OWN + p * CAP
        at = p * 4 * CAP
        twice = 2.0 * received[at + 3 * CAP : at + 4 * CAP, :]
        for c in range(3):
            xyz = received[at + c * CAP : at + c * CAP + CAP, :]
            to = p * BACK + c * CAP
            away[to : to + CAP, :] = twice * (
                xyz * moments[0, from_ : from_ + CAP, :] - moments[1 + c, from_ : from_ + CAP, :]
            )
    back_copies = []
    for p in BACK_ORDER:
        offset = OFFSETS[p]
        copy = pltpu.make_async_remote_copy(
            src_ref=away.at[pl.ds(p * BACK, BACK)],
            dst_ref=back.at[pl.ds(p * BACK, BACK)],
            send_sem=back_send.at[p],
            recv_sem=back_recv.at[p],
            device_id=sp_peer(offset),
            device_id_type=MESH,
        )
        copy.start()
        back_copies.append(copy)
    collect(OWN, 0)
    twice = 2.0 * weights[0:OWN, :]
    for c in range(3):
        force_ref[c] = twice * (coords[c] * moments[0, 0:OWN, :] - moments[1 + c, 0:OWN, :])
    sent = [send_rows[pl.ds(lax.rem(me + 16 - offset, 16), 1), :] for offset in OFFSETS]
    hot = one_hot(OWN, 0, jnp.concatenate(sent + [jnp.full((1, 128 - HALO), -1, I32)], axis=1))
    hots[:, :128] = hot
    hots[:, 128:] = hot
    for copy in back_copies:
        copy.wait()
    for c in range(3):
        rows = [back[p * BACK + c * CAP : p * BACK + c * CAP + CAP, :] for p in range(len(OFFSETS))]
        hi, lo = two_pieces(jnp.concatenate(rows + [jnp.zeros((128 - HALO, 128), F32)], axis=0))
        force_ref[c] += jnp.dot(
            hots[...], jnp.concatenate([hi, lo], axis=0), preferred_element_type=F32
        )


def restraint(*given):
    dma = pltpu.SemaphoreType.DMA
    peers = len(OFFSETS)
    tiles = pltpu.VMEM((TILES, 128), F32)
    return pl.pallas_call(
        restraint_kernel,
        out_shape=(
            jax.ShapeDtypeStruct((3, OWN, 128), F32),
            jax.ShapeDtypeStruct((TILES, 128), F32),
        ),
        in_specs=[HBM] * 9,
        out_specs=(VMEM,) * 2,
        scratch_shapes=[
            pltpu.VMEM((3, OWN, 128), F32),
            pltpu.VMEM((ROWS, 128), F32),
            pltpu.VMEM((3, TILES, 128), F32),
            tiles,
            tiles,
            tiles,
            pltpu.VMEM((TILES, LIST), I32),
            pltpu.VMEM((1, TILES), I32),
            pltpu.VMEM((16, CAP), I32),
            pltpu.SMEM((16, CAP), I32),
            pltpu.VMEM((TILES, LIST), I32),
            pltpu.VMEM((BATCHES, PAIRS_OF), I32),
            pltpu.SMEM((TILES, LIST), I32),
            pltpu.VMEM((4 * HALO, 128), F32),
            pltpu.VMEM((4 * HALO, 128), F32),
            pltpu.VMEM((ROWS, 16, 128), BF),
            pltpu.VMEM((TILES, 128, DEPTH), BF),
            pltpu.VMEM((TILES * DEPTH, 128), F32),
            pltpu.VMEM(((LAG + 1) * STEPS_OF, 128, 256), F32),
            pltpu.VMEM((TILES_OF, 128, 128), F32),
            pltpu.VMEM((GROUPS, TILES_OF, 128), F32),
            pltpu.VMEM((8, GROUPS, TILES_OF, 128), F32),
            pltpu.VMEM((GROUPS, TILES_OF, 128), F32),
            pltpu.VMEM((TILES * LIST, 4, 128), F32),
            pltpu.VMEM((4, TABLE, 128), F32),
            pltpu.VMEM((3 * HALO, 128), F32),
            pltpu.VMEM((3 * HALO, 128), F32),
            pltpu.VMEM((OWN, 256), BF),
            dma((13,)),
            dma((peers,)),
            dma((peers,)),
            dma((GROUPS, 7)),
            dma((GROUPS, 7)),
            dma((peers,)),
            dma((peers,)),
        ],
        compiler_params=params(53, 0),
        name="restraint",
    )(*given)


def store_kernel(force_ref, mean_ref, force_hbm, mean_hbm, sems):
    copies = [pltpu.make_async_copy(mean_ref, mean_hbm, sems.at[0])]
    for c in range(3):
        for h in range(2):
            rows = pl.ds(OWN // 2 * h, OWN // 2)
            copies.append(
                pltpu.make_async_copy(
                    force_ref.at[c, rows], force_hbm.at[c, rows], sems.at[1 + 2 * c + h]
                )
            )
    for copy in copies:
        copy.start()
    for copy in copies:
        copy.wait()


def store(forces, mean):
    return pl.pallas_call(
        store_kernel,
        out_shape=(
            jax.ShapeDtypeStruct((3, OWN, 128), F32),
            jax.ShapeDtypeStruct((TILES, 128), F32),
        ),
        in_specs=[VMEM] * 2,
        out_specs=(HBM,) * 2,
        scratch_shapes=[pltpu.SemaphoreType.DMA((7,))],
        compiler_params=params(2),
        name="store",
    )(forces, mean)


def local(
    coords, atom_weight, centers, inv_width, density, variance, tile_blocks, tile_counts, send_blocks
):
    own, send = jnp.transpose(coords[0], (1, 0, 2)), send_blocks[0]
    centers = jnp.transpose(centers, (1, 0, 2))
    given = (send, own, atom_weight, tile_blocks, tile_counts[None], centers, inv_width, density, variance)
    forces, mean = store(
        *restraint(*[pltpu.with_memory_space_constraint(x, pltpu.HBM) for x in given])
    )
    return jnp.transpose(forces, (1, 0, 2))[None], mean


def solution(mesh):
    return jax.shard_map(
        local,
        mesh=mesh,
        in_specs=(
            P("rep", "sp", None, None),
            P("sp", None),
            P("sp", None, None),
            P("sp", None),
            P("sp", None),
            P("sp", None),
            P("sp", None),
            P("sp"),
            P("sp", None, None),
        ),
        out_specs=(P("rep", "sp", None, None), P("sp", None)),
        check_vma=False,
    )
```

```python
import functools

import jax
import jax.numpy as jnp
from jax import lax
from jax.experimental import pallas as pl
from jax.experimental.pallas import tpu as pltpu
from jax.sharding import PartitionSpec as P

MESH = pl.DeviceIdType.MESH
BF = jnp.bfloat16
F32 = jnp.float32
I32 = jnp.int32
VMEM = pl.BlockSpec(memory_space=pltpu.VMEM)
SMEM = pl.BlockSpec(memory_space=pltpu.SMEM)
HBM = pl.BlockSpec(memory_space=pltpu.HBM)

OFFSETS = (1, 2, 3, 8, 13, 14, 15)
CAP = 16
SENT_ORDER = (0, 1, 2, 3, 4, 5, 6)
WAIT_ORDER = (0, 6, 3, 2, 4, 1, 5)
BACK_ORDER = (1, 0, 2, 3, 5, 4, 6)
OWN = 512
HALO = len(OFFSETS) * CAP
TABLE = OWN + HALO
DUMMY = TABLE
ROWS = TABLE + CAP
TILES = 32
LIST = 32
STEPS = TILES * LIST // 2
GROUPS = 8
LAG = 5
TILES_OF = TILES // GROUPS
STEPS_OF = STEPS // GROUPS
PAIRS_OF = 256
BATCHES = TILES * LIST // PAIRS_OF
BACK = 3 * CAP
DEPTH = 48
LOG2E = 1.4426950408889634


def params(limit_mib, collective_id=None):
    more = {} if collective_id is None else {"collective_id": collective_id, "has_side_effects": True}
    return pltpu.CompilerParams(vmem_limit_bytes=limit_mib << 20, **more)


def sp_peer(offset):
    return (lax.axis_index("rep"), lax.rem(lax.axis_index("sp") + offset, 16))


def pieces(x):
    hi = x.astype(BF).astype(F32)
    rest = x - hi
    mid = rest.astype(BF).astype(F32)
    return hi, mid, rest - mid


def put_features(xyz, feats, first, lines, at):
    square = xyz[0] * xyz[0] + xyz[1] * xyz[1] + xyz[2] * xyz[2]
    for row, value in enumerate((*xyz, square)):
        hi, mid, lo = pieces(value)
        for group, piece in enumerate((hi, mid, hi, lo)):
            lines[pl.ds(at * 128 + 4 * group + row, 8, stride=16), :] = piece
    for b in range(8):
        feats[first + b] = lines[at * 128 + 16 * b : at * 128 + 16 * b + 16, :].astype(BF)


def put_rates(centers, width, rates, lines):
    slope = width[...] * LOG2E
    x = [centers[c] for c in range(3)]
    size = x[0] * x[0] + x[1] * x[1] + x[2] * x[2]
    zero = jnp.zeros((TILES, 128), F32)
    rows = [zero] * DEPTH
    for c, value in enumerate([2.0 * slope * x[0], 2.0 * slope * x[1], 2.0 * slope * x[2], -slope]):
        hi, mid, lo = pieces(value)
        for group, piece in enumerate((hi, hi, mid, hi, lo, mid)):
            rows[4 * group + c] = piece
    for at, piece in enumerate(pieces(-slope * size)):
        rows[32 + at] = piece
    for r in range(DEPTH):
        for q in range(TILES // 8):
            lines[pl.ds(8 * q * DEPTH + r, 8, stride=DEPTH), :] = rows[r][8 * q : 8 * q + 8]

    def tile(t, carry):
        block = lines[pl.ds(pl.multiple_of(t * DEPTH, 8), DEPTH), :]
        rates[t] = jnp.transpose(block).astype(BF)
        return carry

    lax.fori_loop(0, TILES, tile, 0, unroll=4)


def table_ids(lists, counts, ids):
    me = lax.axis_index("sp")
    named = lists[...]
    slot = named - OWN
    offset = (lax.shift_right_arithmetic(slot, 4) - me) & 15
    place = jnp.where(offset < 4, offset - 1, jnp.where(offset == 8, 3, offset - 9))
    named = jnp.where(slot < 0, named, OWN + place * CAP + (slot & (CAP - 1)))
    row = jnp.broadcast_to(counts[...], (TILES, TILES)).astype(F32)
    sub = lax.broadcasted_iota(I32, (TILES, TILES), 0)
    lane = lax.broadcasted_iota(I32, (TILES, TILES), 1)
    count = jnp.sum(jnp.where(lane == sub, row, 0.0), axis=1, keepdims=True)
    ids[...] = jnp.where(lane.astype(F32) < count, named, DUMMY)


def two_pieces(x):
    hi = x.astype(BF)
    return hi, (x - hi.astype(F32)).astype(BF)


def one_hot(rows, first, names):
    at = lax.broadcasted_iota(I32, (rows, names.shape[1]), 0) + first
    return jnp.where(at == names, 1.0, 0.0).astype(BF)


def restraint_kernel(
    send_hbm, coords_hbm, weight_hbm, lists_hbm, counts_hbm, centers_hbm, width_hbm, density_hbm, variance_hbm,
    force_ref, mean_ref,
    coords, weights, centers, width, density, variance, lists, counts, send_rows, send_ref,
    ids, names, ids_smem, pack, received, feats, rates, lines, power, total, model, slots, means,
    entries, moments, away, back, hots,
    near_sem, halo_send, halo_recv, rep_send, rep_recv, back_send, back_recv,
):
    rep, me = lax.axis_index("rep"), lax.axis_index("sp")
    rep_peers = [(lax.rem(rep + d, 8), me) for d in range(1, 8)]
    barrier = pltpu.get_barrier_semaphore()
    for peer in [sp_peer(o) for o in OFFSETS] + rep_peers:
        pl.semaphore_signal(barrier, inc=1, device_id=peer, device_id_type=MESH)
    near = [
        pltpu.make_async_copy(src, dst, near_sem.at[i])
        for i, (src, dst) in enumerate((
            (send_hbm, send_ref),
            (coords_hbm.at[0], coords.at[0]),
            (coords_hbm.at[1], coords.at[1]),
            (coords_hbm.at[2], coords.at[2]),
            (weight_hbm, weights.at[pl.ds(0, OWN)]),
            (lists_hbm, lists),
            (counts_hbm, counts),
            (centers_hbm, centers),
            (width_hbm, width),
            (density_hbm, density),
            (variance_hbm, variance),
            (send_hbm, send_rows),
        ))
    ]
    for copy in near:
        copy.start()
    for copy in near[:5]:
        copy.wait()

    halo_copies = {}
    for p in SENT_ORDER:
        offset = OFFSETS[p]
        to = lax.rem(me + 16 - offset, 16)
        for k in range(CAP):
            b = send_ref[to, k]
            for c in range(3):
                row = (p * 4 + c) * CAP + k
                pack[row : row + 1, :] = coords[c, pl.ds(b, 1), :]
            row = (p * 4 + 3) * CAP + k
            pack[row : row + 1, :] = weights[pl.ds(b, 1), :]
    pl.semaphore_wait(barrier, len(OFFSETS) + 7)
    for p in SENT_ORDER:
        offset = OFFSETS[p]
        copy = pltpu.make_async_remote_copy(
            src_ref=pack.at[pl.ds(p * 4 * CAP, 4 * CAP)],
            dst_ref=received.at[pl.ds(p * 4 * CAP, 4 * CAP)],
            send_sem=halo_send.at[p],
            recv_sem=halo_recv.at[p],
            device_id=sp_peer(16 - offset),
            device_id_type=MESH,
        )
        copy.start()
        halo_copies[p] = copy

    for copy in near[5:]:
        copy.wait()
    table_ids(lists, counts, ids)
    to_smem = pltpu.make_async_copy(ids, ids_smem, near_sem.at[12])
    to_smem.start()
    put_rates(centers, width, rates, lines)
    for t in range(TILES):
        g, j = divmod(t, PAIRS_OF // LIST)
        names[g : g + 1, LIST * j : LIST * j + LIST] = ids[t : t + 1, :]
    weights[TABLE:ROWS, :] = jnp.zeros((ROWS - TABLE, 128), F32)
    for b in range(TABLE, ROWS):
        feats[b] = jnp.zeros((16, 128), BF)

    def own_features(i, carry):
        for u in range(4):
            b = pl.multiple_of(32 * i + 8 * u, 8)
            put_features([coords[c, pl.ds(b, 8), :] for c in range(3)], feats, b, lines, u)
        return carry

    lax.fori_loop(0, OWN // 32, own_features, 0)
    to_smem.wait()
    for p in WAIT_ORDER:
        halo_copies[p].wait()
        for h in range(CAP // 8):
            rows = [
                received[(p * 4 + c) * CAP + 8 * h : (p * 4 + c) * CAP + 8 * h + 8, :]
                for c in range(4)
            ]
            first = OWN + p * CAP + 8 * h
            put_features(rows[:3], feats, first, lines, (2 * p + h) % 4)
            weights[first : first + 8, :] = rows[3]
    lines[0 : TILES_OF * 16, :] = jnp.zeros((TILES_OF * 16, 128), F32)
    ones = jnp.ones((16, 256), BF)

    def replicas(group):
        return [
            pltpu.make_async_remote_copy(
                src_ref=model.at[group],
                dst_ref=slots.at[rep, group],
                send_sem=rep_send.at[group, d],
                recv_sem=rep_recv.at[group, d],
                device_id=peer,
                device_id_type=MESH,
            )
            for d, peer in enumerate(rep_peers)
        ]

    def place_of(group):
        return STEPS_OF * lax.rem(group, LAG)

    def first_step(group, place, j, s):
        tile = TILES_OF * group + j
        b1, b2 = ids_smem[tile, 2 * s], ids_smem[tile, 2 * s + 1]
        pair = jnp.concatenate([feats[b1], feats[b2]], axis=1)
        rows = jnp.concatenate([pair, pair, ones], axis=0)
        k = jnp.exp2(jnp.dot(rates[tile], rows, preferred_element_type=F32))
        power[place + j * (LIST // 2) + s] = k
        more = k[:, :128] * weights[pl.ds(b1, 1), :] + k[:, 128:] * weights[pl.ds(b2, 1), :]
        if s == 0:
            total[j] = more
        else:
            total[j] += more

    def send_model(group):
        for j in range(TILES_OF):
            model[group, j : j + 1, :] = jnp.sum(total[j], axis=-1)[None, :]
        for copy in replicas(group):
            copy.start()

    def pulls_of(group):
        rows = pl.ds(pl.multiple_of(TILES_OF * group, TILES_OF), TILES_OF)
        slots[rep, group] = model[group]
        for copy in replicas(group):
            copy.wait()
        sum_ = slots[0, group]
        for r in range(1, 8):
            sum_ = sum_ + slots[r, group]
        mean = sum_ * 0.125
        means[group] = mean
        rate = (mean - density[rows, :]) / variance[rows, :] * width[rows, :]
        for row, value in enumerate([rate] + [rate * centers[c, rows] for c in range(3)]):
            hi = value.astype(BF).astype(F32)
            lines[pl.ds(row, TILES_OF, stride=16), :] = hi
            lines[pl.ds(4 + row, TILES_OF, stride=16), :] = value - hi
        eights = [lines[16 * j : 16 * j + 16, :].astype(BF) for j in range(TILES_OF)]
        return [jnp.concatenate([eight, eight], axis=1) for eight in eights]

    def second_step(group, place, pulls, j, s):
        hi, lo = two_pieces(power[place + j * (LIST // 2) + s])
        both = jnp.dot(pulls[j], jnp.concatenate([hi, lo], axis=0), preferred_element_type=F32)
        four = both[:4] + both[4:8]
        at = (TILES_OF * group + j) * LIST + 2 * s
        entries[at] = four[:, :128]
        entries[at + 1] = four[:, 128:]

    steps = [(j, s) for j in range(TILES_OF) for s in range(LIST // 2)]

    def early(i, carry):
        place = place_of(i)
        for j, s in steps:
            first_step(i, place, j, s)
        send_model(i)
        return carry

    def middle(i, carry):
        pulls = pulls_of(i - LAG)
        place = place_of(i)
        for j, s in steps:
            second_step(i - LAG, place, pulls, j, s)
            first_step(i, place, j, s)
        send_model(i)
        return carry

    def late(i, carry):
        pulls = pulls_of(i - LAG)
        place = place_of(i)
        for j, s in steps:
            second_step(i - LAG, place, pulls, j, s)
        return carry

    lax.fori_loop(0, LAG, early, 0)
    lax.fori_loop(LAG, GROUPS, middle, 0)
    lax.fori_loop(GROUPS, GROUPS + LAG, late, 0)
    for g in range(GROUPS):
        mean_ref[TILES_OF * g : TILES_OF * g + TILES_OF, :] = means[g]

    def collect(rows, first):
        def body(g, carry):
            hot = one_hot(rows, first, names[pl.ds(g, 1), :])
            for half in range(2):
                parts = []
                for c in (2 * half, 2 * half + 1):
                    x = sum_rows(g, c)
                    parts.append(two_pieces(x))
                hi = jnp.concatenate([parts[0][0], parts[1][0]], axis=1)
                lo = jnp.concatenate([parts[0][1], parts[1][1]], axis=1)
                got = jnp.dot(hot, hi, preferred_element_type=F32) + jnp.dot(
                    hot, lo, preferred_element_type=F32
                )
                for q in range(2):
                    moments[2 * half + q, first : first + rows, :] += got[:, 128 * q : 128 * q + 128]
            return carry

        def sum_rows(g, c):
            flat = entries.reshape(TILES * LIST * 4, 128)
            return flat[pl.ds(pl.multiple_of(g * PAIRS_OF * 4, 8) + c, PAIRS_OF, stride=4), :]

        for c in range(4):
            moments[c, first : first + rows, :] = jnp.zeros((rows, 128), F32)
        lax.fori_loop(0, BATCHES, body, 0)

    collect(HALO, OWN)
    for p in range(len(OFFSETS)):
        from_ = OWN + p * CAP
        at = p * 4 * CAP
        twice = 2.0 * received[at + 3 * CAP : at + 4 * CAP, :]
        for c in range(3):
            xyz = received[at + c * CAP : at + c * CAP + CAP, :]
            to = p * BACK + c * CAP
            away[to : to + CAP, :] = twice * (
                xyz * moments[0, from_ : from_ + CAP, :] - moments[1 + c, from_ : from_ + CAP, :]
            )
    back_copies = []
    for p in BACK_ORDER:
        offset = OFFSETS[p]
        copy = pltpu.make_async_remote_copy(
            src_ref=away.at[pl.ds(p * BACK, BACK)],
            dst_ref=back.at[pl.ds(p * BACK, BACK)],
            send_sem=back_send.at[p],
            recv_sem=back_recv.at[p],
            device_id=sp_peer(offset),
            device_id_type=MESH,
        )
        copy.start()
        back_copies.append(copy)
    collect(OWN, 0)
    twice = 2.0 * weights[0:OWN, :]
    for c in range(3):
        force_ref[c] = twice * (coords[c] * moments[0, 0:OWN, :] - moments[1 + c, 0:OWN, :])
    sent = [send_rows[pl.ds(lax.rem(me + 16 - offset, 16), 1), :] for offset in OFFSETS]
    hot = one_hot(OWN, 0, jnp.concatenate(sent + [jnp.full((1, 128 - HALO), -1, I32)], axis=1))
    hots[:, :128] = hot
    hots[:, 128:] = hot
    for copy in back_copies:
        copy.wait()
    for c in range(3):
        rows = [back[p * BACK + c * CAP : p * BACK + c * CAP + CAP, :] for p in range(len(OFFSETS))]
        hi, lo = two_pieces(jnp.concatenate(rows + [jnp.zeros((128 - HALO, 128), F32)], axis=0))
        force_ref[c] += jnp.dot(
            hots[...], jnp.concatenate([hi, lo], axis=0), preferred_element_type=F32
        )


def restraint(*given):
    dma = pltpu.SemaphoreType.DMA
    peers = len(OFFSETS)
    tiles = pltpu.VMEM((TILES, 128), F32)
    return pl.pallas_call(
        restraint_kernel,
        out_shape=(
            jax.ShapeDtypeStruct((3, OWN, 128), F32),
            jax.ShapeDtypeStruct((TILES, 128), F32),
        ),
        in_specs=[HBM] * 9,
        out_specs=(VMEM,) * 2,
        scratch_shapes=[
            pltpu.VMEM((3, OWN, 128), F32),
            pltpu.VMEM((ROWS, 128), F32),
            pltpu.VMEM((3, TILES, 128), F32),
            tiles,
            tiles,
            tiles,
            pltpu.VMEM((TILES, LIST), I32),
            pltpu.VMEM((1, TILES), I32),
            pltpu.VMEM((16, CAP), I32),
            pltpu.SMEM((16, CAP), I32),
            pltpu.VMEM((TILES, LIST), I32),
            pltpu.VMEM((BATCHES, PAIRS_OF), I32),
            pltpu.SMEM((TILES, LIST), I32),
            pltpu.VMEM((4 * HALO, 128), F32),
            pltpu.VMEM((4 * HALO, 128), F32),
            pltpu.VMEM((ROWS, 16, 128), BF),
            pltpu.VMEM((TILES, 128, DEPTH), BF),
            pltpu.VMEM((TILES * DEPTH, 128), F32),
            pltpu.VMEM((LAG * STEPS_OF, 128, 256), F32),
            pltpu.VMEM((TILES_OF, 128, 128), F32),
            pltpu.VMEM((GROUPS, TILES_OF, 128), F32),
            pltpu.VMEM((8, GROUPS, TILES_OF, 128), F32),
            pltpu.VMEM((GROUPS, TILES_OF, 128), F32),
            pltpu.VMEM((TILES * LIST, 4, 128), F32),
            pltpu.VMEM((4, TABLE, 128), F32),
            pltpu.VMEM((3 * HALO, 128), F32),
            pltpu.VMEM((3 * HALO, 128), F32),
            pltpu.VMEM((OWN, 256), BF),
            dma((13,)),
            dma((peers,)),
            dma((peers,)),
            dma((GROUPS, 7)),
            dma((GROUPS, 7)),
            dma((peers,)),
            dma((peers,)),
        ],
        compiler_params=params(53, 0),
        name="restraint",
    )(*given)


def store_kernel(force_ref, mean_ref, force_hbm, mean_hbm, sems):
    copies = [pltpu.make_async_copy(mean_ref, mean_hbm, sems.at[0])]
    for c in range(3):
        for h in range(2):
            rows = pl.ds(OWN // 2 * h, OWN // 2)
            copies.append(
                pltpu.make_async_copy(
                    force_ref.at[c, rows], force_hbm.at[c, rows], sems.at[1 + 2 * c + h]
                )
            )
    for copy in copies:
        copy.start()
    for copy in copies:
        copy.wait()


def store(forces, mean):
    return pl.pallas_call(
        store_kernel,
        out_shape=(
            jax.ShapeDtypeStruct((3, OWN, 128), F32),
            jax.ShapeDtypeStruct((TILES, 128), F32),
        ),
        in_specs=[VMEM] * 2,
        out_specs=(HBM,) * 2,
        scratch_shapes=[pltpu.SemaphoreType.DMA((7,))],
        compiler_params=params(2),
        name="store",
    )(forces, mean)


def local(
    coords, atom_weight, centers, inv_width, density, variance, tile_blocks, tile_counts, send_blocks
):
    own, send = jnp.transpose(coords[0], (1, 0, 2)), send_blocks[0]
    centers = jnp.transpose(centers, (1, 0, 2))
    given = (send, own, atom_weight, tile_blocks, tile_counts[None], centers, inv_width, density, variance)
    forces, mean = store(
        *restraint(*[pltpu.with_memory_space_constraint(x, pltpu.HBM) for x in given])
    )
    return jnp.transpose(forces, (1, 0, 2))[None], mean


def solution(mesh):
    return jax.shard_map(
        local,
        mesh=mesh,
        in_specs=(
            P("rep", "sp", None, None),
            P("sp", None),
            P("sp", None, None),
            P("sp", None),
            P("sp", None),
            P("sp", None),
            P("sp", None),
            P("sp"),
            P("sp", None, None),
        ),
        out_specs=(P("rep", "sp", None, None), P("sp", None)),
        check_vma=False,
    )
```
